32 devices in a mesh: dp: 16 (over z, x, core), tensor: 2 (over y).
Axes of the slice: x: 2, y: 2, z: 4, core: 2. Of those that a mesh axis runs over, the one named last changes fastest.
Arguments:
- tokens: bfloat16 [1024, 48, 1152], P('tensor', 'dp'), may hold values from -6 to 6
- conditioning: bfloat16 [29, 1152], replicated, may hold values from -6 to 6
- cotangent: bfloat16 [1024, 48, 1152], P('tensor', 'dp'), may hold values from -6 to 6
- latent_counts: int32 [16], replicated, may hold values from 0 to 3, as said below
- latent_order: int32 [29], replicated, may hold values from 0 to 28, each once
- w_ada: bfloat16 [1152, 6, 1152], P('dp', None, 'tensor'), may hold values from -0.1875 to 0.1875
- b_ada: bfloat16 [6, 1152], replicated, may hold values from -3 to 3
- w_qkv: bfloat16 [1152, 3, 1152], P('dp', None, 'tensor'), may hold values from -0.1875 to 0.1875
- b_qv: bfloat16 [2, 1152], replicated, may hold values from -3 to 3
- w_out: bfloat16 [1152, 1152], P('tensor', 'dp'), may hold values from -3 to 3
- w_fc1: bfloat16 [1152, 4608], P('dp', 'tensor'), may hold values from -0.1875 to 0.1875
- b_fc1: bfloat16 [4608], replicated, may hold values from -3 to 3
- w_fc2: bfloat16 [4608, 1152], P('tensor', 'dp'), may hold values from -0.375 to 0.375
- b_out2: bfloat16 [2, 1152], replicated, may hold values from -3 to 3
Outputs:
- out_tokens: bfloat16 [1024, 48, 1152], P('tensor', 'dp')
- grad_tokens: bfloat16 [1024, 48, 1152], P('tensor', 'dp')
- grad_cond: float32 [29, 1152], replicated
- grad_w_ada: float32 [1152, 6, 1152], P('dp', None, 'tensor')
- grad_b_ada: float32 [6, 1152], replicated
- grad_w_qkv: float32 [1152, 3, 1152], P('dp', None, 'tensor')
- grad_b_qv: float32 [2, 1152], replicated
- grad_w_out: float32 [1152, 1152], P('tensor', 'dp')
- grad_w_fc1: float32 [1152, 4608], P('dp', 'tensor')
- grad_b_fc1: float32 [4608], replicated
- grad_w_fc2: float32 [4608, 1152], P('tensor', 'dp')
- grad_b_out2: float32 [2, 1152], replicated
The draws below stay inside these ranges and needn't reach their ends.
Inputs may be any that keep to these rules, and one draw needn't show every extreme that they name: latent_counts[r] is the number of latents held by index r of dp; they sum to 29, and some index holds 3. Each latent once. Index r of dp holds latent_order[c], ..., latent_order[c + latent_counts[r] - 1] in its first slots, c the sum of latent_counts over lower indices; tokens and cotangent of its other slots are not used.
All inputs are finite; a program needn't handle non-finite values.
Results may differ from the reference program's by a relative error of at most 0.015.
The reference program's roundings to bfloat16 on the way count: a program that leaves them out, or rounds other values in their place, can miss the bound.
Values may be sent and summed in bfloat16 or wider, within the bound.
No kernel may reach another device: no remote copies, remote signals or barrier semaphores. Data moves between devices by JAX's collectives and lax.ppermute only.
A program may use at most 320 MiB of HBM per device.

```python
import jax
import jax.numpy as jnp
from jax import lax

D = 1152
HEADS = 16
HEAD_DIM = 72
FF = 4608
SEQ = 1024
SLOTS = 3
LATENTS = 29
SLOTS_ALL = 48
N_DP = 16


def draw_latent_counts(key, part):
    key = jax.random.fold_in(key, 11)
    first_key, second_key = jax.random.split(key)
    full_rank = jax.random.randint(first_key, (), 0, N_DP).astype(jnp.int32)
    others = jax.random.permutation(second_key, SLOTS * (N_DP - 1))[:LATENTS - SLOTS].astype(jnp.int32)
    owner = others // SLOTS
    owner = owner + (owner >= full_rank).astype(jnp.int32)
    ranks = jnp.arange(N_DP, dtype=jnp.int32)
    counts = jnp.sum((owner[:, None] == ranks[None, :]).astype(jnp.int32), axis=0)
    return (counts + SLOTS * (ranks == full_rank).astype(jnp.int32)).astype(jnp.int32)


def steps_of(key, extent, pieces, smallest, top_value):
    def one(position, blocks):
        draws = jax.random.uniform(jax.random.fold_in(jax.random.fold_in(key, 6), position), (blocks,), jnp.float32, smallest / len(pieces), top_value / len(pieces))
        return jnp.repeat(jnp.exp(draws), extent[position] // blocks).reshape((-1,) + (1,) * (len(extent) - position - 1))

    gain = one(*pieces[0])
    for cut in pieces[1:]:
        gain = gain * one(*cut)
    return gain


def normal_values(stream_key, dims, scale, bound, shards=(), kind=jnp.bfloat16):
    entries = scale * jax.random.normal(stream_key, dims, jnp.float32)
    if shards:
        entries = entries * steps_of(stream_key, dims, shards, -0.22, 0.18)
    return jnp.clip(entries, -bound, bound).astype(kind)


def setup_inputs(seed: int = 0) -> dict:
    key_list = jax.random.split(jax.random.key(seed), 15)
    tokens = normal_values(key_list[0], (SEQ, SLOTS_ALL, D), 1.0, 6.0, ((0, 2), (1, 16)))
    conditioning = normal_values(key_list[1], (LATENTS, D), 1.0, 6.0)
    cotangent = normal_values(key_list[2], (SEQ, SLOTS_ALL, D), 1.0, 6.0, ((0, 2), (1, 16)))
    latent_counts = draw_latent_counts(jax.random.fold_in(key_list[14], 71), 0)
    latent_order = jax.random.permutation(key_list[4], LATENTS).astype(jnp.int32)
    w_ada = normal_values(key_list[5], (D, 6, D), D ** -0.5, 0.1875, ((0, 16), (2, 2)))
    b_ada = normal_values(key_list[6], (6, D), 0.5, 3.0)
    w_qkv = normal_values(key_list[7], (D, 3, D), D ** -0.5, 0.1875, ((0, 16), (2, 2)))
    b_qv = normal_values(key_list[8], (2, D), 0.5, 3.0)
    w_out = normal_values(key_list[9], (D, D), (max(1, D // 256)) ** -0.5, 3.0, ((0, 2), (1, 16)))
    w_fc1 = normal_values(key_list[10], (D, FF), D ** -0.5, 0.1875, ((0, 16), (1, 2)))
    b_fc1 = normal_values(key_list[11], (FF,), 0.5, 3.0)
    w_fc2 = normal_values(key_list[12], (FF, D), (max(1, FF // 16)) ** -0.5, 0.375, ((0, 2), (1, 16)))
    b_out2 = normal_values(key_list[13], (2, D), 0.5, 3.0)
    return dict(tokens=tokens, conditioning=conditioning, cotangent=cotangent, latent_counts=latent_counts, latent_order=latent_order, w_ada=w_ada, b_ada=b_ada, w_qkv=w_qkv, b_qv=b_qv, w_out=w_out, w_fc1=w_fc1, b_fc1=b_fc1, w_fc2=w_fc2, b_out2=b_out2)


EPSILON = 1e-06

@jax.custom_vjp
def low(v):
    return lax.optimization_barrier(v.astype(jnp.bfloat16)).astype(jnp.float32)

@jax.custom_vjp
def low_back(v):
    return v

def low_keep(v):
    return (low(v), None)

def low_pass(kept, grad):
    return (grad,)

def back_keep(v):
    return (v, None)

def back_low(kept, grad):
    return (low(grad),)
low.defvjp(low_keep, low_pass)
low_back.defvjp(back_keep, back_low)

def product(form, left, right):
    return jnp.einsum(form, left, right, precision=lax.Precision.HIGHEST)

def layer_norm(values):
    center = values - lax.optimization_barrier(jnp.mean(values, axis=-1, keepdims=True))
    spread = lax.optimization_barrier(jnp.mean(center * center, axis=-1, keepdims=True))
    return center * lax.rsqrt(spread + EPSILON)

def attend(items):
    query, keys_all, values = items
    query = query.reshape(SEQ, HEADS, HEAD_DIM)
    keys_all = keys_all.reshape(SEQ, HEADS, HEAD_DIM)
    values = values.reshape(SEQ, HEADS, HEAD_DIM)
    scores = low_back(product('qhd,khd->hqk', query, keys_all) * HEAD_DIM ** (-0.5))
    peak = lax.optimization_barrier(jnp.max(scores, axis=-1, keepdims=True))
    expo = jnp.exp(scores - peak)
    probs = low(expo / lax.optimization_barrier(jnp.sum(expo, axis=-1, keepdims=True)))
    mixed = product('hqk,khd->qhd', probs, values)
    return low(low_back(mixed.reshape(SEQ, D)))

def layer(params, tokens_group, picker_group, live_group):
    conditioning, w_ada, b_ada, w_qkv, b_qv, w_out, w_fc1, b_fc1, w_fc2, b_out2 = params
    cond_rows = product('gl,ld->gd', picker_group, conditioning)
    cond_silu = low(jax.nn.silu(cond_rows))
    modulation = product('gd,djc->gjc', cond_silu, w_ada) + b_ada
    shift_attn = modulation[:, 0][:, None]
    scale_attn = modulation[:, 1][:, None]
    gate_attn = modulation[:, 2][:, None]
    shift_mlp = modulation[:, 3][:, None]
    scale_mlp = modulation[:, 4][:, None]
    gate_mlp = modulation[:, 5][:, None]
    mixed_attn = low(layer_norm(tokens_group) * (1.0 + scale_attn) + shift_attn)
    projected = product('gsd,dkc->gskc', mixed_attn, w_qkv)
    query = low(low_back(projected[:, :, 0] + b_qv[0]))
    keys_all = low(low_back(projected[:, :, 1]))
    values = low(low_back(projected[:, :, 2] + b_qv[1]))
    attn_mixed = lax.map(jax.checkpoint(attend), (query, keys_all, values))
    branch_attn = low_back(product('gsc,cd->gsd', attn_mixed, w_out) + b_out2[0])
    middle = tokens_group + gate_attn * branch_attn
    mixed_mlp = low(layer_norm(middle) * (1.0 + scale_mlp) + shift_mlp)
    pre_act = low_back(product('gsd,df->gsf', mixed_mlp, w_fc1) + b_fc1)
    hidden = low(jax.nn.gelu(pre_act, approximate=True))
    branch_mlp = low_back(product('gsf,fd->gsd', hidden, w_fc2) + b_out2[1])
    return (middle + gate_mlp * branch_mlp) * live_group[:, None, None]

def reference(tokens, conditioning, cotangent, latent_counts, latent_order, w_ada, b_ada, w_qkv, b_qv, w_out, w_fc1, b_fc1, w_fc2, b_out2):
    slots_all = SLOTS * N_DP
    starts = jnp.cumsum(latent_counts) - latent_counts
    slot_index = jnp.arange(slots_all, dtype=jnp.int32)
    owner = (slot_index // SLOTS).astype(jnp.int32)
    within = (slot_index % SLOTS).astype(jnp.int32)
    live = (within < latent_counts[owner]).astype(jnp.float32)
    chosen = latent_order[jnp.clip(starts[owner] + within, 0, LATENTS - 1)]
    picker = (chosen[:, None] == jnp.arange(LATENTS, dtype=jnp.int32)[None, :]).astype(jnp.float32)
    params = tuple((array.astype(jnp.float32) for array in (conditioning, w_ada, b_ada, w_qkv, b_qv, w_out, w_fc1, b_fc1, w_fc2, b_out2)))
    group = 4
    groups = slots_all // group
    tokens_grouped = jnp.swapaxes(tokens.astype(jnp.float32), 0, 1).reshape(groups, group, SEQ, D)
    cot_grouped = jnp.swapaxes(cotangent.astype(jnp.float32), 0, 1).reshape(groups, group, SEQ, D)
    picker_grouped = picker.reshape(groups, group, LATENTS)
    live_grouped = live.reshape(groups, group)

    def step(totals, items):
        tokens_group, cot_group, picker_group, live_group = items

        def forward(params_now, tokens_now):
            return layer(params_now, tokens_now, picker_group, live_group)
        output, pullback = jax.vjp(forward, params, tokens_group)
        grad_params, grad_group = pullback(cot_group)
        totals = jax.tree.map(jnp.add, totals, grad_params)
        return (totals, (output, grad_group))
    zeros = jax.tree.map(jnp.zeros_like, params)
    totals, (outputs, grads_in) = lax.scan(step, zeros, (tokens_grouped, cot_grouped, picker_grouped, live_grouped))
    out_tokens = jnp.swapaxes(outputs.reshape(slots_all, SEQ, D), 0, 1).astype(jnp.bfloat16)
    grad_tokens = jnp.swapaxes(grads_in.reshape(slots_all, SEQ, D), 0, 1).astype(jnp.bfloat16)
    return (out_tokens, grad_tokens, totals[0], totals[1], totals[2], totals[3], totals[4], totals[5], totals[6], totals[7], totals[8], totals[9])
```

```python
from functools import partial

import jax
import jax.numpy as jnp
import numpy as np
from jax import lax
from jax.experimental import pallas as pl
from jax.experimental.pallas import tpu as pltpu
from jax.sharding import Mesh
from jax.sharding import PartitionSpec as P

HEADS = 16
HEAD_DIM = 72
EPSILON = 1e-06
WINDOW = 256
LANES = 128
LOG2E = 1.4426950408889634
VMEM_BYTES = 56 * 2**20

NN = (((1,), (0,)), ((), ()))
NT = (((1,), (1,)), ((), ()))
TN = (((0,), (0,)), ((), ()))


def dot(left, right, dims=NN):
    return lax.dot_general(left, right, dims, preferred_element_type=jnp.float32)


def norm_parts(values):
    center = values - jnp.mean(values, axis=-1, keepdims=True)
    spread = jnp.mean(center * center, axis=-1, keepdims=True)
    inverse = lax.rsqrt(spread + EPSILON)
    return center * inverse, inverse


def norm_back(normed, inverse, grad):
    mean_grad = jnp.mean(grad, axis=-1, keepdims=True)
    mean_prod = jnp.mean(grad * normed, axis=-1, keepdims=True)
    return (grad - mean_grad - normed * mean_prod) * inverse


def round_up(value, step):
    return -(-value // step) * step


def window(column, width):
    start = jnp.minimum((column // LANES) * LANES, width - WINDOW)
    low = column - start
    lane = lax.broadcasted_iota(jnp.int32, (1, WINDOW), 1)
    return pl.ds(pl.multiple_of(start, LANES), WINDOW), (lane >= low) & (lane < low + HEAD_DIM)


def forward_kernel(k_at, v_at, chunk, q_ref, kv_ref, o_ref, log_ref):
    head = pl.program_id(0)
    column = head * HEAD_DIM
    q_cols, _ = window(column, q_ref.shape[1])
    k_cols, _ = window(k_at + column, kv_ref.shape[1])
    v_cols, v_mask = window(v_at + column, kv_ref.shape[1])
    o_cols, o_mask = window(column, o_ref.shape[1])

    @pl.when(head == 0)
    def _():
        o_ref[...] = jnp.zeros_like(o_ref)

    keys = align_head(kv_ref[:, k_cols], k_at + column, kv_ref.shape[1], column, q_ref.shape[1])
    values = align_head(kv_ref[:, v_cols], v_at + column, kv_ref.shape[1], column, o_ref.shape[1])
    factor = HEAD_DIM ** (-0.5) * LOG2E
    for part in range(q_ref.shape[0] // chunk):
        rows = pl.ds(part * chunk, chunk)
        scores = dot(keys, q_ref[rows, q_cols], NT)
        peak = jnp.max(scores, axis=0, keepdims=True)
        expo = jnp.exp2((scores - peak) * factor)
        total = jnp.sum(expo, axis=0, keepdims=True)
        mixed = dot(values, expo.astype(jnp.bfloat16), TN) * (1.0 / total)
        o_ref[rows, o_cols] = o_ref[rows, o_cols] + mixed.T.astype(jnp.bfloat16)
        log_ref[pl.ds(head, 1), rows] = peak * factor + jnp.log2(total)


def align_head(block, from_column, from_width, to_column, to_width):
    from_start = jnp.minimum((from_column // LANES) * LANES, from_width - WINDOW)
    to_start = jnp.minimum((to_column // LANES) * LANES, to_width - WINDOW)
    from_low = from_column - from_start
    to_low = to_column - to_start
    shift = lax.rem(to_low - from_low + WINDOW, WINDOW)
    lane = lax.broadcasted_iota(jnp.int32, (1, WINDOW), 1)
    moved = pltpu.roll(block.astype(jnp.float32), shift, 1)
    keep = (lane >= to_low) & (lane < to_low + HEAD_DIM)
    return jnp.where(keep, moved, 0.0).astype(jnp.bfloat16)


def backward_kernel(k_at, v_at, dk_at, dv_at, chunk, joined, q_ref, kv_ref, do_ref, log_ref, *outs):
    head = pl.program_id(0)
    column = head * HEAD_DIM
    if joined:
        (dq_ref,) = outs
        dkv_ref = dq_ref
    else:
        dq_ref, dkv_ref = outs
    q_cols, q_mask = window(column, q_ref.shape[1])
    k_cols, _ = window(k_at + column, kv_ref.shape[1])
    v_cols, _ = window(v_at + column, kv_ref.shape[1])
    do_cols, _ = window(column, do_ref.shape[1])
    dq_cols, dq_mask = window(column, dq_ref.shape[1])
    dk_cols, dk_mask = window(dk_at + column, dkv_ref.shape[1])
    dv_cols, dv_mask = window(dv_at + column, dkv_ref.shape[1])

    @pl.when(head == 0)
    def _():
        for out in outs:
            out[...] = jnp.zeros_like(out)

    width = q_ref.shape[1]
    keys = align_head(kv_ref[:, k_cols], k_at + column, kv_ref.shape[1], column, width)
    values = align_head(kv_ref[:, v_cols], v_at + column, kv_ref.shape[1], column, do_ref.shape[1])
    scale = HEAD_DIM ** (-0.5)
    factor = scale * LOG2E
    dk_total = jnp.zeros((kv_ref.shape[0], WINDOW), jnp.float32)
    dv_total = jnp.zeros((kv_ref.shape[0], WINDOW), jnp.float32)
    for part in range(q_ref.shape[0] // chunk):
        rows = pl.ds(part * chunk, chunk)
        query = q_ref[rows, q_cols]
        grad = do_ref[rows, do_cols]
        scores = dot(keys, query, NT)
        probs = jnp.exp2(scores * factor - log_ref[pl.ds(head, 1), rows])
        d_probs = dot(values, grad, NT)
        inner = jnp.sum(d_probs * probs, axis=0, keepdims=True)
        d_scores = (probs * (d_probs - inner)).astype(jnp.bfloat16)
        dv_total = dv_total + dot(probs.astype(jnp.bfloat16), grad)
        dk_total = dk_total + dot(d_scores, query)
        d_query = (dot(keys, d_scores, TN) * scale).T
        moved = move_head(d_query, column, width, column, dq_ref.shape[1])
        dq_ref[rows, dq_cols] = dq_ref[rows, dq_cols] + moved
    dk_ref_add(dkv_ref, dk_cols, move_head(dk_total * scale, column, width, dk_at + column, dkv_ref.shape[1]))
    dk_ref_add(dkv_ref, dv_cols, move_head(dv_total, column, do_ref.shape[1], dv_at + column, dkv_ref.shape[1]))


def dk_ref_add(ref, cols, values):
    ref[:, cols] = ref[:, cols] + values


def move_head(block, from_column, from_width, to_column, to_width):
    return align_head(block, from_column, from_width, to_column, to_width)


def spec(shape, *index):
    return pl.BlockSpec(shape, lambda head: index, pipeline_mode=pl.Buffered(1))


def attend_forward(q, q_block, kv, kv_block, k_at, v_at, rows, keys, heads):
    width = round_up(heads * HEAD_DIM, LANES)
    return pl.pallas_call(
        partial(forward_kernel, k_at, v_at, min(256, rows)),
        grid=(heads,),
        in_specs=[
            spec((rows, q.shape[1]), q_block, 0),
            spec((keys, kv.shape[1]), kv_block, 0),
        ],
        out_specs=[spec((rows, width), 0, 0), spec((heads, rows), 0, 0)],
        out_shape=[
            jax.ShapeDtypeStruct((rows, width), jnp.bfloat16),
            jax.ShapeDtypeStruct((heads, rows), jnp.float32),
        ],
        compiler_params=pltpu.CompilerParams(vmem_limit_bytes=VMEM_BYTES),
        cost_estimate=pl.CostEstimate(
            flops=4 * heads * rows * keys * WINDOW,
            bytes_accessed=2 * (rows + keys) * 1792,
            transcendentals=heads * rows * keys,
        ),
        name="attend_forward",
    )(q, kv)


def attend_backward(q, q_block, kv, kv_block, k_at, v_at, grad, grad_block, log_total, rows, keys, heads, joined):
    slab = heads * HEAD_DIM
    if joined:
        out_specs = [spec((rows, q.shape[1]), 0, 0)]
        out_shape = [jax.ShapeDtypeStruct((rows, q.shape[1]), jnp.bfloat16)]
        dk_at, dv_at = k_at, v_at
    else:
        width = round_up(slab, LANES)
        out_specs = [spec((rows, width), 0, 0), spec((keys, 2 * slab), 0, 0)]
        out_shape = [
            jax.ShapeDtypeStruct((rows, width), jnp.bfloat16),
            jax.ShapeDtypeStruct((keys, 2 * slab), jnp.bfloat16),
        ]
        dk_at, dv_at = 0, slab
    return pl.pallas_call(
        partial(backward_kernel, k_at, v_at, dk_at, dv_at, min(256, rows), joined),
        grid=(heads,),
        in_specs=[
            spec((rows, q.shape[1]), q_block, 0),
            spec((keys, kv.shape[1]), kv_block, 0),
            spec((rows, grad.shape[1]), grad_block, 0),
            spec((heads, rows), 0, 0),
        ],
        out_specs=out_specs,
        out_shape=out_shape,
        compiler_params=pltpu.CompilerParams(vmem_limit_bytes=VMEM_BYTES),
        cost_estimate=pl.CostEstimate(
            flops=10 * heads * rows * keys * WINDOW,
            bytes_accessed=4 * (rows + keys) * 1792,
            transcendentals=heads * rows * keys,
        ),
        name="attend_backward",
    )(q, kv, grad, log_total)


def per_device(
    tokens,
    conditioning,
    cotangent,
    latent_counts,
    latent_order,
    w_ada,
    b_ada,
    w_qkv,
    b_qv,
    w_out,
    w_fc1,
    b_fc1,
    w_fc2,
    b_out2,
):
    tsize = lax.axis_size("tensor")
    t = lax.axis_index("tensor")
    c = lax.axis_index("core")
    r = lax.axis_index("dpo") * 2 + c
    dp_size = lax.axis_size("dpo") * 2
    f32, bf16 = jnp.float32, jnp.bfloat16
    rows, slots, width = tokens.shape
    latents = conditioning.shape[0]
    drows = w_ada.shape[0]
    slab = width // tsize
    half_heads = HEADS // 2
    hslab = half_heads * HEAD_DIM
    head_w = slab // 2
    fc_w = w_fc1.shape[1] // 2
    qkv_w = round_up(3 * hslab, LANES)
    out_w = round_up(hslab, LANES)
    pair = tsize == 2 and slots == 3

    def swap_core(x):
        return lax.ppermute(x, "core", [(0, 1), (1, 0)])

    def swap_tensor(x):
        return lax.ppermute(x, "tensor", [(0, 1), (1, 0)])

    def in_order(index, mine, other, axis):
        first = jnp.where(index == 0, mine, other)
        second = jnp.where(index == 0, other, mine)
        return jnp.concatenate([first, second], axis=axis)

    def at(x, index, axis):
        return lax.dynamic_index_in_dim(x, index, axis, keepdims=False)

    starts = jnp.cumsum(latent_counts) - latent_counts
    slot_all = jnp.arange(slots * dp_size, dtype=jnp.int32)
    owner, within = slot_all // slots, slot_all % slots
    live_all = (within < latent_counts[owner]).astype(f32)
    chosen = latent_order[jnp.clip(starts[owner] + within, 0, latents - 1)]
    picker = (chosen[:, None] == jnp.arange(latents, dtype=jnp.int32)[None, :]).astype(f32)
    picker_live = picker * live_all[:, None]
    cond_here = lax.dynamic_slice_in_dim(conditioning, r * drows, drows, 1).astype(f32)
    silu_here = jax.nn.silu(cond_here).astype(bf16)
    silu_slots = jnp.dot(picker, silu_here.astype(f32), precision=lax.Precision.HIGHEST).astype(bf16)

    ada_flat = w_ada.reshape(drows, 6 * slab)
    mod_part = dot(silu_slots, ada_flat)
    mod_here = lax.psum_scatter(mod_part, ("dpo", "core"), scatter_dimension=0, tiled=True)
    mod_here = mod_here.reshape(slots, 6, slab)
    if tsize == 2:
        modulation = in_order(t, mod_here, swap_tensor(mod_here), 2)
    else:
        modulation = lax.all_gather(mod_here, "tensor", axis=2, tiled=True)
    modulation = modulation + b_ada.astype(f32)[None]

    if pair:

        def take(x):
            mine = at(x, t, 1)
            other = swap_tensor(at(x, 1 - t, 1))
            return jnp.concatenate([mine, other, x[:, 2]], axis=0)

        group_slots = jnp.stack([t, t, jnp.full_like(t, 2)])
    else:

        def take(x):
            return jnp.swapaxes(x, 0, 1).reshape(slots * rows, width)

        group_slots = jnp.arange(slots, dtype=jnp.int32)
    groups = slots
    count = groups * rows
    tokens_in = take(tokens)
    cot_in = take(cotangent)
    slot_pick = group_slots[:, None] == jnp.arange(slots, dtype=jnp.int32)[None, :]
    live_here = lax.dynamic_slice_in_dim(live_all, r * slots, slots, 0)
    live = jnp.sum(jnp.where(slot_pick, live_here[None], 0.0), axis=1)
    mod_groups = jnp.sum(
        jnp.where(slot_pick[:, :, None, None], modulation[None], 0.0), axis=1
    )

    def grouped(x):
        return x.reshape(groups, rows, x.shape[-1])

    def flat(x):
        return x.reshape(count, x.shape[-1])

    shift_attn, scale_attn, gate_attn, shift_mlp, scale_mlp, gate_mlp = (
        mod_groups[:, i][:, None, :] for i in range(6)
    )

    shards = (
        w_qkv.reshape(drows, 3, 2, head_w),
        w_out.T.reshape(drows, 1, 2, head_w),
        w_fc1.reshape(drows, 1, 2, fc_w),
        w_fc2.T.reshape(drows, 1, 2, fc_w),
    )
    pads = (qkv_w - 3 * hslab, out_w - hslab, 0, 0)

    def side(which):
        return jnp.concatenate([at(x, which, 2).reshape(drows, -1) for x in shards], axis=1)

    both = in_order(c, side(c), swap_core(side(1 - c)), 0)
    if tsize == 2:
        met = swap_tensor(both)
        by_tensor = [jnp.where(t == 0, both, met), jnp.where(t == 0, met, both)]
    else:
        met = lax.all_gather(both, "tensor", axis=0, tiled=False)
        by_tensor = [met[i] for i in range(tsize)]
    gathered = []
    offset = 0
    for x, pad in zip(shards, pads):
        kinds, wide = x.shape[1], x.shape[3]
        parts = [
            y[:, offset : offset + kinds * wide].reshape(2 * drows, kinds, 1, wide) for y in by_tensor
        ]
        offset += kinds * wide
        joined = jnp.concatenate(parts, axis=2).reshape(2 * drows, kinds * tsize * wide)
        if pad:
            joined = jnp.pad(joined, ((0, 0), (0, pad)))
        own = lax.all_gather(joined, "dpo", axis=0, tiled=True)
        gathered.append((own, swap_core(own)))
    qkv_ws, out_ws, fc1_ws, fc2_ws = gathered

    def bias_halves(bias, wide):
        parts = bias.astype(f32).reshape(bias.shape[0], tsize, 2, wide)
        return [at(parts, which, 2).reshape(bias.shape[0], tsize * wide) for which in (c, 1 - c)]

    qv_halves = bias_halves(b_qv, head_w)
    qkv_bias = [
        jnp.concatenate(
            [b[0], jnp.zeros((hslab,), f32), b[1], jnp.zeros((pads[0],), f32)]
        )
        for b in qv_halves
    ]
    fc1_bias = [b[0] for b in bias_halves(b_fc1[None], fc_w)]
    bias_attn_out, bias_mlp_out = b_out2[0].astype(f32), b_out2[1].astype(f32)

    x_in = grouped(tokens_in.astype(f32))
    norm_attn, inv_attn = norm_parts(x_in)
    mixed_attn = flat((norm_attn * (1.0 + scale_attn) + shift_attn).astype(bf16))
    qkv = [(dot(mixed_attn, w) + b).astype(bf16) for w, b in zip(qkv_ws, qkv_bias)]

    if pair:
        segments = [(2, 1)]
    else:
        segments = [(g, 1) for g in range(groups)]
    seq = rows * tsize

    def gather_keys(x):
        if tsize == 2:
            return jnp.concatenate([x, swap_tensor(x)], axis=0)
        return lax.all_gather(x, "tensor", axis=0, tiled=True)

    def scatter_keys(x):
        if tsize == 2:
            return (x[:rows].astype(f32) + swap_tensor(x[rows:]).astype(f32)).astype(bf16)
        return lax.psum_scatter(x.astype(f32), "tensor", scatter_dimension=0, tiled=True).astype(bf16)

    mixed_parts, log_parts, key_parts = [], [], []
    for x in qkv:
        keys_by_segment = [
            gather_keys(x[g * rows : (g + 1) * rows, hslab : 3 * hslab]) for g, _ in segments
        ]
        outs, logs = [], []
        if pair:
            out, log = attend_forward(x, 0, x, 0, hslab, 2 * hslab, seq, seq, half_heads)
            outs.append(out)
            logs.append(log)
        for (g, _), kv in zip(segments, keys_by_segment):
            out, log = attend_forward(x, g, kv, 0, 0, hslab, rows, seq, half_heads)
            outs.append(out)
            logs.append(log)
        mixed_parts.append(jnp.concatenate(outs, axis=0))
        log_parts.append(logs)
        key_parts.append(keys_by_segment)
    branch_attn = grouped(
        sum(dot(x, w, NT) for x, w in zip(mixed_parts, out_ws)) + bias_attn_out
    )
    middle = x_in + gate_attn * branch_attn
    norm_mlp, inv_mlp = norm_parts(middle)
    mixed_mlp = flat((norm_mlp * (1.0 + scale_mlp) + shift_mlp).astype(bf16))

    grad_out = grouped(cot_in.astype(f32)) * live[:, None, None]
    d_branch_mlp = flat((grad_out * gate_mlp).astype(bf16))
    hidden, d_pre, grad_fc1, grad_fc2, d_bias_fc1 = [], [], [], [], []
    for w1, w2, b in zip(fc1_ws, fc2_ws, fc1_bias):
        pre_act = dot(mixed_mlp, w1) + b
        act = jax.nn.gelu(pre_act, approximate=True).astype(bf16)
        d_hidden = dot(d_branch_mlp, w2)
        _, gelu_back = jax.vjp(partial(jax.nn.gelu, approximate=True), pre_act)
        d_act = gelu_back(d_hidden)[0].astype(bf16)
        hidden.append(act)
        d_pre.append(d_act)
        grad_fc1.append(dot(mixed_mlp, d_act, TN).astype(bf16))
        grad_fc2.append(dot(d_branch_mlp, act, TN).astype(bf16))
        d_bias_fc1.append(jnp.sum(d_act.astype(f32), axis=0))
    branch_mlp = grouped(sum(dot(h, w, NT) for h, w in zip(hidden, fc2_ws)) + bias_mlp_out)
    out_rows = flat(((middle + gate_mlp * branch_mlp) * live[:, None, None]).astype(bf16))
    d_gate_mlp = jnp.sum(grad_out * branch_mlp, axis=1)
    d_mixed_mlp = grouped(sum(dot(g, w, NT) for g, w in zip(d_pre, fc1_ws)))
    d_shift_mlp = jnp.sum(d_mixed_mlp, axis=1)
    d_scale_mlp = jnp.sum(d_mixed_mlp * norm_mlp, axis=1)
    d_middle = grad_out + norm_back(norm_mlp, inv_mlp, d_mixed_mlp * (1.0 + scale_mlp))
    d_branch_attn = flat((d_middle * gate_attn).astype(bf16))
    d_gate_attn = jnp.sum(d_middle * branch_attn, axis=1)

    d_qkv = []
    grad_out_w = []
    for x, w, mixed, logs, keys_by_segment in zip(qkv, out_ws, mixed_parts, log_parts, key_parts):
        d_mixed = dot(d_branch_attn, w).astype(bf16)
        grad_out_w.append(dot(d_branch_attn, mixed, TN).astype(bf16))
        d_rows = []
        first = 1 if pair else 0
        for i, (g, _) in enumerate(segments):
            d_q, d_kv = attend_backward(
                x, g, keys_by_segment[i], 0, 0, hslab, d_mixed, g, logs[first + i], rows, seq, half_heads, False
            )
            d_rows.append(
                jnp.concatenate(
                    [d_q[:, :hslab], scatter_keys(d_kv), jnp.zeros((rows, pads[0]), bf16)], axis=1
                )
            )
        if pair:
            (whole,) = attend_backward(
                x, 0, x, 0, hslab, 2 * hslab, d_mixed, 0, logs[0], seq, seq, half_heads, True
            )
            d_rows.insert(0, whole)
        d_qkv.append(jnp.concatenate(d_rows, axis=0))
    grad_qkv = [dot(mixed_attn, d, TN).astype(bf16) for d in d_qkv]
    d_mixed_attn = grouped(sum(dot(d, w, NT) for d, w in zip(d_qkv, qkv_ws)))
    d_shift_attn = jnp.sum(d_mixed_attn, axis=1)
    d_scale_attn = jnp.sum(d_mixed_attn * norm_attn, axis=1)
    grad_rows = flat(
        (d_middle + norm_back(norm_attn, inv_attn, d_mixed_attn * (1.0 + scale_attn))).astype(bf16)
    )

    def give(x):
        if not pair:
            return jnp.swapaxes(x.reshape(slots, rows, width), 0, 1)
        mine, other, last = x[:rows], swap_tensor(x[rows : 2 * rows]), x[2 * rows :]
        return jnp.stack(
            [jnp.where(t == 0, mine, other), jnp.where(t == 0, other, mine), last], axis=1
        )

    out_tokens = give(out_rows)
    grad_tokens = give(grad_rows)

    def scatter_weight(halves, kinds, wide):
        own, other = halves
        total = (own.astype(f32) + swap_core(other).astype(f32)).astype(bf16)
        part = lax.optimization_barrier(
            lax.psum_scatter(total, "dpo", scatter_dimension=0, tiled=True)
        )
        part = part[:, : kinds * tsize * wide].reshape(2 * drows, kinds, tsize, wide)
        if tsize == 2:
            met = swap_tensor(at(part, 1 - t, 2))
            part = at(part, t, 2).astype(f32) + met.astype(f32)
        else:
            part = lax.psum_scatter(part.astype(f32), "tensor", scatter_dimension=2, tiled=True)
            part = part.reshape(2 * drows, kinds, wide)
        part = part.reshape(2, drows, kinds, 1, wide)
        mine = at(part, c, 0)
        met = swap_core(at(part, 1 - c, 0))
        return in_order(c, mine, met, 2).reshape(drows, kinds, 2 * wide)

    grad_w_fc1 = scatter_weight(grad_fc1, 1, fc_w).reshape(drows, 2 * fc_w)
    grad_w_fc2 = scatter_weight(grad_fc2, 1, fc_w).reshape(drows, 2 * fc_w).T
    grad_w_out = scatter_weight(grad_out_w, 1, head_w).reshape(drows, slab).T
    grad_w_qkv = scatter_weight(grad_qkv, 3, head_w)

    d_mod_groups = jnp.stack(
        [d_shift_attn, d_scale_attn, d_gate_attn, d_shift_mlp, d_scale_mlp, d_gate_mlp], axis=1
    )
    d_mod = jnp.sum(
        jnp.where(slot_pick[:, :, None, None], d_mod_groups[:, None], 0.0), axis=0
    )

    def bias_back(halves, wide):
        own, other = (x.reshape(x.shape[0], tsize, 1, wide) for x in halves)
        return in_order(c, own, other, 2).reshape(own.shape[0], tsize, 2 * wide)

    d_bias_q = [jnp.sum(d[:, :hslab].astype(f32), axis=0) for d in d_qkv]
    d_bias_v = [jnp.sum(d[:, 2 * hslab : 3 * hslab].astype(f32), axis=0) for d in d_qkv]
    d_bias_qv = bias_back([jnp.stack([q, v]) for q, v in zip(d_bias_q, d_bias_v)], head_w)
    d_bias_fc = bias_back([x[None] for x in d_bias_fc1], fc_w)
    d_bias_out = jnp.stack(
        [jnp.sum(d_branch_attn.astype(f32), axis=0), jnp.sum(d_branch_mlp.astype(f32), axis=0)]
    ).reshape(2, tsize, slab)
    small = jnp.concatenate(
        [
            jnp.swapaxes(d_mod.reshape(slots * 6, tsize, slab), 0, 1).reshape(tsize, -1),
            jnp.swapaxes(d_bias_qv, 0, 1).reshape(tsize, -1),
            jnp.swapaxes(d_bias_fc, 0, 1).reshape(tsize, -1),
            jnp.swapaxes(d_bias_out, 0, 1).reshape(tsize, -1),
        ],
        axis=1,
    )
    if tsize == 2:
        small = at(small, t, 0) + swap_tensor(at(small, 1 - t, 0))
    else:
        small = lax.psum_scatter(small, "tensor", scatter_dimension=0, tiled=True)[0]
    every = lax.all_gather(small, ("dpo", "core"), axis=0, tiled=False)
    mod_size = slots * 6 * slab
    mod_all = every[:, :mod_size].reshape(dp_size * slots, 6 * slab)
    bias_sum = jnp.sum(every[:, mod_size:], axis=0)
    d_ada_bias = jnp.sum(mod_all, axis=0)
    grad_w_ada = lax.dot_general(
        silu_slots.astype(f32), mod_all, TN, precision=lax.Precision.HIGHEST
    ).reshape(drows, 6, slab)
    d_silu_slots = lax.dot_general(
        mod_all, ada_flat.astype(f32), NT, precision=lax.Precision.HIGHEST
    )
    d_silu = lax.dot_general(picker_live, d_silu_slots, TN, precision=lax.Precision.HIGHEST)
    _, silu_back = jax.vjp(jax.nn.silu, cond_here)
    cond_part = silu_back(d_silu)[0].reshape(-1)
    shared = jnp.concatenate([d_ada_bias, bias_sum])
    share = shared.shape[0] // dp_size
    shared_part = lax.dynamic_slice_in_dim(shared, r * share, share, 0)
    last = lax.all_gather(
        jnp.concatenate([cond_part, shared_part]), ("dpo", "core", "tensor"), axis=0, tiled=False
    ).reshape(dp_size, tsize, -1)
    cond_size = latents * drows
    grad_cond = jnp.sum(last[:, :, :cond_size], axis=1).reshape(dp_size, latents, drows)
    grad_cond = jnp.swapaxes(grad_cond, 0, 1).reshape(latents, width)
    spread = jnp.swapaxes(last[:, :, cond_size:], 0, 1).reshape(tsize, dp_size * share)

    def whole(start, kinds, wide):
        part = spread[:, start : start + kinds * wide].reshape(tsize, kinds, wide)
        return jnp.swapaxes(part, 0, 1).reshape(kinds, tsize * wide)

    grad_b_ada = whole(0, 6, slab)
    grad_b_qv = whole(6 * slab, 2, slab)
    grad_b_fc1 = whole(8 * slab, 1, 2 * fc_w)[0]
    grad_b_out2 = whole(8 * slab + 2 * fc_w, 2, slab)
    return (
        out_tokens,
        grad_tokens,
        grad_cond,
        grad_w_ada,
        grad_b_ada,
        grad_w_qkv,
        grad_b_qv,
        grad_w_out,
        grad_w_fc1,
        grad_b_fc1,
        grad_w_fc2,
        grad_b_out2,
    )


def solution(mesh):
    dp_size, tensor_size = mesh.devices.shape
    split = Mesh(mesh.devices.reshape(dp_size // 2, 2, tensor_size), ("dpo", "core", "tensor"))
    dp = ("dpo", "core")
    placed = (
        P("tensor", dp, None),
        P(),
        P("tensor", dp, None),
        P(),
        P(),
        P(dp, None, "tensor"),
        P(),
        P(dp, None, "tensor"),
        P(),
        P("tensor", dp),
        P(dp, "tensor"),
        P(),
        P("tensor", dp),
        P(),
    )
    return jax.shard_map(
        per_device,
        mesh=split,
        in_specs=placed,
        out_specs=(
            P("tensor", dp, None),
            P("tensor", dp, None),
            P(),
            P(dp, None, "tensor"),
            P(),
            P(dp, None, "tensor"),
            P(),
            P("tensor", dp),
            P(dp, "tensor"),
            P(),
            P("tensor", dp),
            P(),
        ),
        check_vma=False,
    )
```

```python
from functools import partial

import jax
import jax.numpy as jnp
import numpy as np
from jax import lax
from jax.experimental import pallas as pl
from jax.experimental.pallas import tpu as pltpu
from jax.sharding import Mesh
from jax.sharding import PartitionSpec as P

HEADS = 16
HEAD_DIM = 72
EPSILON = 1e-06
WINDOW = 256
LANES = 128
LOG2E = 1.4426950408889634
VMEM_BYTES = 56 * 2**20

NN = (((1,), (0,)), ((), ()))
NT = (((1,), (1,)), ((), ()))
TN = (((0,), (0,)), ((), ()))


def dot(left, right, dims=NN):
    return lax.dot_general(left, right, dims, preferred_element_type=jnp.float32)


def norm_parts(values):
    center = values - jnp.mean(values, axis=-1, keepdims=True)
    spread = jnp.mean(center * center, axis=-1, keepdims=True)
    inverse = lax.rsqrt(spread + EPSILON)
    return center * inverse, inverse


def norm_back(normed, inverse, grad):
    mean_grad = jnp.mean(grad, axis=-1, keepdims=True)
    mean_prod = jnp.mean(grad * normed, axis=-1, keepdims=True)
    return (grad - mean_grad - normed * mean_prod) * inverse


def round_up(value, step):
    return -(-value // step) * step


def window(column, width):
    start = jnp.minimum((column // LANES) * LANES, width - WINDOW)
    low = column - start
    lane = lax.broadcasted_iota(jnp.int32, (1, WINDOW), 1)
    return pl.ds(pl.multiple_of(start, LANES), WINDOW), (lane >= low) & (lane < low + HEAD_DIM)


def forward_kernel(k_at, v_at, chunk, q_ref, kv_ref, o_ref, log_ref):
    head = pl.program_id(0)
    column = head * HEAD_DIM
    q_cols, _ = window(column, q_ref.shape[1])
    k_cols, _ = window(k_at + column, kv_ref.shape[1])
    v_cols, v_mask = window(v_at + column, kv_ref.shape[1])
    o_cols, o_mask = window(column, o_ref.shape[1])

    @pl.when(head == 0)
    def _():
        o_ref[...] = jnp.zeros_like(o_ref)

    keys = align_head(kv_ref[:, k_cols], k_at + column, kv_ref.shape[1], column, q_ref.shape[1])
    values = align_head(kv_ref[:, v_cols], v_at + column, kv_ref.shape[1], column, o_ref.shape[1])
    factor = HEAD_DIM ** (-0.5) * LOG2E
    for part in range(q_ref.shape[0] // chunk):
        rows = pl.ds(part * chunk, chunk)
        scores = dot(keys, q_ref[rows, q_cols], NT)
        peak = jnp.max(scores, axis=0, keepdims=True)
        expo = jnp.exp2((scores - peak) * factor)
        total = jnp.sum(expo, axis=0, keepdims=True)
        mixed = dot(values, expo.astype(jnp.bfloat16), TN) * (1.0 / total)
        o_ref[rows, o_cols] = o_ref[rows, o_cols] + mixed.T.astype(jnp.bfloat16)
        log_ref[pl.ds(head, 1), rows] = peak * factor + jnp.log2(total)


def align_head(block, from_column, from_width, to_column, to_width):
    from_start = jnp.minimum((from_column // LANES) * LANES, from_width - WINDOW)
    to_start = jnp.minimum((to_column // LANES) * LANES, to_width - WINDOW)
    from_low = from_column - from_start
    to_low = to_column - to_start
    shift = lax.rem(to_low - from_low + WINDOW, WINDOW)
    lane = lax.broadcasted_iota(jnp.int32, (1, WINDOW), 1)
    moved = pltpu.roll(block.astype(jnp.float32), shift, 1)
    keep = (lane >= to_low) & (lane < to_low + HEAD_DIM)
    return jnp.where(keep, moved, 0.0).astype(jnp.bfloat16)


def backward_kernel(k_at, v_at, dk_at, dv_at, chunk, joined, q_ref, kv_ref, do_ref, log_ref, *outs):
    head = pl.program_id(0)
    column = head * HEAD_DIM
    if joined:
        (dq_ref,) = outs
        dkv_ref = dq_ref
    else:
        dq_ref, dkv_ref = outs
    q_cols, q_mask = window(column, q_ref.shape[1])
    k_cols, _ = window(k_at + column, kv_ref.shape[1])
    v_cols, _ = window(v_at + column, kv_ref.shape[1])
    do_cols, _ = window(column, do_ref.shape[1])
    dq_cols, dq_mask = window(column, dq_ref.shape[1])
    dk_cols, dk_mask = window(dk_at + column, dkv_ref.shape[1])
    dv_cols, dv_mask = window(dv_at + column, dkv_ref.shape[1])

    @pl.when(head == 0)
    def _():
        for out in outs:
            out[...] = jnp.zeros_like(out)

    width = q_ref.shape[1]
    keys = align_head(kv_ref[:, k_cols], k_at + column, kv_ref.shape[1], column, width)
    values = align_head(kv_ref[:, v_cols], v_at + column, kv_ref.shape[1], column, do_ref.shape[1])
    scale = HEAD_DIM ** (-0.5)
    factor = scale * LOG2E
    dk_total = jnp.zeros((kv_ref.shape[0], WINDOW), jnp.float32)
    dv_total = jnp.zeros((kv_ref.shape[0], WINDOW), jnp.float32)
    for part in range(q_ref.shape[0] // chunk):
        rows = pl.ds(part * chunk, chunk)
        query = q_ref[rows, q_cols]
        grad = do_ref[rows, do_cols]
        scores = dot(keys, query, NT)
        probs = jnp.exp2(scores * factor - log_ref[pl.ds(head, 1), rows])
        d_probs = dot(values, grad, NT)
        inner = jnp.sum(d_probs * probs, axis=0, keepdims=True)
        d_scores = (probs * (d_probs - inner)).astype(jnp.bfloat16)
        dv_total = dv_total + dot(probs.astype(jnp.bfloat16), grad)
        dk_total = dk_total + dot(d_scores, query)
        d_query = (dot(keys, d_scores, TN) * scale).T
        moved = move_head(d_query, column, width, column, dq_ref.shape[1])
        dq_ref[rows, dq_cols] = dq_ref[rows, dq_cols] + moved
    dk_ref_add(dkv_ref, dk_cols, move_head(dk_total * scale, column, width, dk_at + column, dkv_ref.shape[1]))
    dk_ref_add(dkv_ref, dv_cols, move_head(dv_total, column, do_ref.shape[1], dv_at + column, dkv_ref.shape[1]))


def dk_ref_add(ref, cols, values):
    ref[:, cols] = ref[:, cols] + values


def move_head(block, from_column, from_width, to_column, to_width):
    return align_head(block, from_column, from_width, to_column, to_width)


def spec(shape, *index):
    return pl.BlockSpec(shape, lambda head: index, pipeline_mode=pl.Buffered(1))


def attend_forward(q, q_block, kv, kv_block, k_at, v_at, rows, keys, heads):
    width = round_up(heads * HEAD_DIM, LANES)
    return pl.pallas_call(
        partial(forward_kernel, k_at, v_at, min(256, rows)),
        grid=(heads,),
        in_specs=[
            spec((rows, q.shape[1]), q_block, 0),
            spec((keys, kv.shape[1]), kv_block, 0),
        ],
        out_specs=[spec((rows, width), 0, 0), spec((heads, rows), 0, 0)],
        out_shape=[
            jax.ShapeDtypeStruct((rows, width), jnp.bfloat16),
            jax.ShapeDtypeStruct((heads, rows), jnp.float32),
        ],
        compiler_params=pltpu.CompilerParams(vmem_limit_bytes=VMEM_BYTES),
        cost_estimate=pl.CostEstimate(
            flops=4 * heads * rows * keys * WINDOW,
            bytes_accessed=2 * (rows + keys) * 1792,
            transcendentals=heads * rows * keys,
        ),
        name="attend_forward",
    )(q, kv)


def attend_backward(q, q_block, kv, kv_block, k_at, v_at, grad, grad_block, log_total, rows, keys, heads, joined):
    slab = heads * HEAD_DIM
    if joined:
        out_specs = [spec((rows, q.shape[1]), 0, 0)]
        out_shape = [jax.ShapeDtypeStruct((rows, q.shape[1]), jnp.bfloat16)]
        dk_at, dv_at = k_at, v_at
    else:
        width = round_up(slab, LANES)
        out_specs = [spec((rows, width), 0, 0), spec((keys, 2 * slab), 0, 0)]
        out_shape = [
            jax.ShapeDtypeStruct((rows, width), jnp.bfloat16),
            jax.ShapeDtypeStruct((keys, 2 * slab), jnp.bfloat16),
        ]
        dk_at, dv_at = 0, slab
    return pl.pallas_call(
        partial(backward_kernel, k_at, v_at, dk_at, dv_at, min(256, rows), joined),
        grid=(heads,),
        in_specs=[
            spec((rows, q.shape[1]), q_block, 0),
            spec((keys, kv.shape[1]), kv_block, 0),
            spec((rows, grad.shape[1]), grad_block, 0),
            spec((heads, rows), 0, 0),
        ],
        out_specs=out_specs,
        out_shape=out_shape,
        compiler_params=pltpu.CompilerParams(vmem_limit_bytes=VMEM_BYTES),
        cost_estimate=pl.CostEstimate(
            flops=10 * heads * rows * keys * WINDOW,
            bytes_accessed=4 * (rows + keys) * 1792,
            transcendentals=heads * rows * keys,
        ),
        name="attend_backward",
    )(q, kv, grad, log_total)


def per_device(
    tokens,
    conditioning,
    cotangent,
    latent_counts,
    latent_order,
    w_ada,
    b_ada,
    w_qkv,
    b_qv,
    w_out,
    w_fc1,
    b_fc1,
    w_fc2,
    b_out2,
):
    tsize = lax.axis_size("tensor")
    t = lax.axis_index("tensor")
    c = lax.axis_index("core")
    r = lax.axis_index("dpo") * 2 + c
    dp_size = lax.axis_size("dpo") * 2
    f32, bf16 = jnp.float32, jnp.bfloat16
    rows, slots, width = tokens.shape
    latents = conditioning.shape[0]
    drows = w_ada.shape[0]
    slab = width // tsize
    half_heads = HEADS // 2
    hslab = half_heads * HEAD_DIM
    head_w = slab // 2
    fc_w = w_fc1.shape[1] // 2
    qkv_w = round_up(3 * hslab, LANES)
    out_w = round_up(hslab, LANES)
    pair = tsize == 2 and slots == 3

    def swap_core(x):
        return lax.ppermute(x, "core", [(0, 1), (1, 0)])

    def swap_tensor(x):
        return lax.ppermute(x, "tensor", [(0, 1), (1, 0)])

    def in_order(index, mine, other, axis):
        first = jnp.where(index == 0, mine, other)
        second = jnp.where(index == 0, other, mine)
        return jnp.concatenate([first, second], axis=axis)

    def at(x, index, axis):
        return lax.dynamic_index_in_dim(x, index, axis, keepdims=False)

    starts = jnp.cumsum(latent_counts) - latent_counts
    slot_all = jnp.arange(slots * dp_size, dtype=jnp.int32)
    owner, within = slot_all // slots, slot_all % slots
    live_all = (within < latent_counts[owner]).astype(f32)
    chosen = latent_order[jnp.clip(starts[owner] + within, 0, latents - 1)]
    picker = (chosen[:, None] == jnp.arange(latents, dtype=jnp.int32)[None, :]).astype(f32)
    picker_live = picker * live_all[:, None]
    cond_here = lax.dynamic_slice_in_dim(conditioning, r * drows, drows, 1).astype(f32)
    silu_here = jax.nn.silu(cond_here).astype(bf16)
    silu_slots = jnp.dot(picker, silu_here.astype(f32), precision=lax.Precision.HIGHEST).astype(bf16)

    ada_flat = w_ada.reshape(drows, 6 * slab)
    mod_part = dot(silu_slots, ada_flat).reshape(dp_size, slots * 6, slab)
    mod_here = lax.psum_scatter(mod_part, ("dpo", "core"), scatter_dimension=0, tiled=True)
    mod_here = mod_here.reshape(slots, 6, slab)
    if tsize == 2:
        modulation = in_order(t, mod_here, swap_tensor(mod_here), 2)
    else:
        modulation = lax.all_gather(mod_here, "tensor", axis=2, tiled=True)
    modulation = modulation + b_ada.astype(f32)[None]

    if pair:

        def take(x):
            mine = at(x, t, 1)
            other = swap_tensor(at(x, 1 - t, 1))
            return jnp.concatenate([mine, other, x[:, 2]], axis=0)

        group_slots = jnp.stack([t, t, jnp.full_like(t, 2)])
    else:

        def take(x):
            return jnp.swapaxes(x, 0, 1).reshape(slots * rows, width)

        group_slots = jnp.arange(slots, dtype=jnp.int32)
    groups = slots
    count = groups * rows
    tokens_in = take(tokens)
    cot_in = take(cotangent)
    slot_pick = group_slots[:, None] == jnp.arange(slots, dtype=jnp.int32)[None, :]
    live_here = lax.dynamic_slice_in_dim(live_all, r * slots, slots, 0)
    live = jnp.sum(jnp.where(slot_pick, live_here[None], 0.0), axis=1)
    mod_groups = jnp.sum(
        jnp.where(slot_pick[:, :, None, None], modulation[None], 0.0), axis=1
    )

    def grouped(x):
        return x.reshape(groups, rows, x.shape[-1])

    def flat(x):
        return x.reshape(count, x.shape[-1])

    shift_attn, scale_attn, gate_attn, shift_mlp, scale_mlp, gate_mlp = (
        mod_groups[:, i][:, None, :] for i in range(6)
    )

    shards = (
        w_qkv.reshape(drows, 3, 2, head_w),
        w_out.T.reshape(drows, 1, 2, head_w),
        w_fc1.reshape(drows, 1, 2, fc_w),
        w_fc2.T.reshape(drows, 1, 2, fc_w),
    )
    pads = (qkv_w - 3 * hslab, out_w - hslab, 0, 0)

    def quad(some):
        def side(which):
            parts = [at(x, which, 2).reshape(drows, -1) for x in some]
            return parts[0] if len(parts) == 1 else jnp.concatenate(parts, axis=1)

        both = in_order(c, side(c), swap_core(side(1 - c)), 0)
        if tsize == 2:
            met = swap_tensor(both)
            return [jnp.where(t == 0, both, met), jnp.where(t == 0, met, both)]
        met = lax.all_gather(both, "tensor", axis=0, tiled=False)
        return [met[i] for i in range(tsize)]

    def columns(by_tensor, offset, kinds, wide, pad):
        parts = [
            y[:, offset : offset + kinds * wide].reshape(2 * drows, kinds, 1, wide) for y in by_tensor
        ]
        joined = jnp.concatenate(parts, axis=2).reshape(2 * drows, kinds * tsize * wide)
        return jnp.pad(joined, ((0, 0), (0, pad))) if pad else joined

    def gather(x):
        own = lax.all_gather(x, "dpo", axis=0, tiled=True)
        return own, swap_core(own)

    qkv_ws = gather(columns(quad(shards[:1]), 0, 3, head_w, pads[0]))
    rest = quad(shards[1:])
    out_fc1 = jnp.concatenate(
        [columns(rest, 0, 1, head_w, pads[1]), columns(rest, head_w, 1, fc_w, 0)], axis=1
    )
    out_fc1_ws = gather(out_fc1)
    out_ws = [w[:, :out_w] for w in out_fc1_ws]
    fc1_ws = [w[:, out_w:] for w in out_fc1_ws]
    first_w, fc2_cols = lax.optimization_barrier(
        (qkv_ws[0], columns(rest, head_w + fc_w, 1, fc_w, 0))
    )
    qkv_ws = (first_w, qkv_ws[1])
    fc2_ws = gather(fc2_cols)

    def bias_halves(bias, wide):
        parts = bias.astype(f32).reshape(bias.shape[0], tsize, 2, wide)
        return [at(parts, which, 2).reshape(bias.shape[0], tsize * wide) for which in (c, 1 - c)]

    qv_halves = bias_halves(b_qv, head_w)
    qkv_bias = [
        jnp.concatenate(
            [b[0], jnp.zeros((hslab,), f32), b[1], jnp.zeros((pads[0],), f32)]
        )
        for b in qv_halves
    ]
    fc1_bias = [b[0] for b in bias_halves(b_fc1[None], fc_w)]
    bias_attn_out, bias_mlp_out = b_out2[0].astype(f32), b_out2[1].astype(f32)

    x_in = grouped(tokens_in.astype(f32))
    norm_attn, inv_attn = norm_parts(x_in)
    mixed_attn = flat((norm_attn * (1.0 + scale_attn) + shift_attn).astype(bf16))
    qkv = [(dot(mixed_attn, w) + b).astype(bf16) for w, b in zip(qkv_ws, qkv_bias)]

    if pair:
        segments = [(2, 1)]
    else:
        segments = [(g, 1) for g in range(groups)]
    seq = rows * tsize

    def gather_keys(x):
        if tsize == 2:
            return jnp.concatenate([x, swap_tensor(x)], axis=0)
        return lax.all_gather(x, "tensor", axis=0, tiled=True)

    def scatter_keys(x):
        if tsize == 2:
            return (x[:rows].astype(f32) + swap_tensor(x[rows:]).astype(f32)).astype(bf16)
        return lax.psum_scatter(x.astype(f32), "tensor", scatter_dimension=0, tiled=True).astype(bf16)

    mixed_parts, log_parts, key_parts = [], [], []
    for x in qkv:
        keys_by_segment = [
            gather_keys(x[g * rows : (g + 1) * rows, hslab : 3 * hslab]) for g, _ in segments
        ]
        outs, logs = [], []
        if pair:
            out, log = attend_forward(x, 0, x, 0, hslab, 2 * hslab, seq, seq, half_heads)
            outs.append(out)
            logs.append(log)
        for (g, _), kv in zip(segments, keys_by_segment):
            out, log = attend_forward(x, g, kv, 0, 0, hslab, rows, seq, half_heads)
            outs.append(out)
            logs.append(log)
        mixed_parts.append(jnp.concatenate(outs, axis=0))
        log_parts.append(logs)
        key_parts.append(keys_by_segment)
    branch_attn = grouped(
        sum(dot(x, w, NT) for x, w in zip(mixed_parts, out_ws)) + bias_attn_out
    )
    middle = x_in + gate_attn * branch_attn
    norm_mlp, inv_mlp = norm_parts(middle)
    mixed_mlp = flat((norm_mlp * (1.0 + scale_mlp) + shift_mlp).astype(bf16))

    grad_out = grouped(cot_in.astype(f32)) * live[:, None, None]
    d_branch_mlp = flat((grad_out * gate_mlp).astype(bf16))
    hidden, d_pre, d_bias_fc1 = [], [], []
    for w1, w2, b in zip(fc1_ws, fc2_ws, fc1_bias):
        pre_act = dot(mixed_mlp, w1) + b
        act = jax.nn.gelu(pre_act, approximate=True).astype(bf16)
        d_hidden = dot(d_branch_mlp, w2)
        _, gelu_back = jax.vjp(partial(jax.nn.gelu, approximate=True), pre_act)
        d_act = gelu_back(d_hidden)[0].astype(bf16)
        hidden.append(act)
        d_pre.append(d_act)
        d_bias_fc1.append(jnp.sum(d_act.astype(f32), axis=0))

    def both_cores(left, rights):
        met = swap_core(dot(left, rights[1], TN).astype(bf16))
        return (dot(left, rights[0], TN).astype(bf16).astype(f32) + met.astype(f32)).astype(bf16)

    total_fc2 = both_cores(d_branch_mlp, hidden)
    total_fc1 = both_cores(mixed_mlp, d_pre)
    hidden, d_pre, total_fc1, total_fc2 = lax.optimization_barrier(
        (hidden, d_pre, total_fc1, total_fc2)
    )
    branch_mlp = grouped(sum(dot(h, w, NT) for h, w in zip(hidden, fc2_ws)) + bias_mlp_out)
    out_rows = flat(((middle + gate_mlp * branch_mlp) * live[:, None, None]).astype(bf16))
    d_gate_mlp = jnp.sum(grad_out * branch_mlp, axis=1)
    d_mixed_mlp = grouped(sum(dot(g, w, NT) for g, w in zip(d_pre, fc1_ws)))
    d_shift_mlp = jnp.sum(d_mixed_mlp, axis=1)
    d_scale_mlp = jnp.sum(d_mixed_mlp * norm_mlp, axis=1)
    d_middle = grad_out + norm_back(norm_mlp, inv_mlp, d_mixed_mlp * (1.0 + scale_mlp))
    d_branch_attn = flat((d_middle * gate_attn).astype(bf16))
    d_gate_attn = jnp.sum(d_middle * branch_attn, axis=1)

    total_out = both_cores(d_branch_attn, mixed_parts)
    d_branch_attn, total_out = lax.optimization_barrier((d_branch_attn, total_out))
    d_qkv = []
    for x, w, logs, keys_by_segment in reversed(list(zip(qkv, out_ws, log_parts, key_parts))):
        d_mixed = dot(d_branch_attn, w).astype(bf16)
        d_rows = []
        first = 1 if pair else 0
        for i, (g, _) in enumerate(segments):
            d_q, d_kv = attend_backward(
                x, g, keys_by_segment[i], 0, 0, hslab, d_mixed, g, logs[first + i], rows, seq, half_heads, False
            )
            d_rows.append(
                jnp.concatenate(
                    [d_q[:, :hslab], scatter_keys(d_kv), jnp.zeros((rows, pads[0]), bf16)], axis=1
                )
            )
        if pair:
            (whole,) = attend_backward(
                x, 0, x, 0, hslab, 2 * hslab, d_mixed, 0, logs[0], seq, seq, half_heads, True
            )
            d_rows.insert(0, whole)
        d_qkv.append(jnp.concatenate(d_rows, axis=0))
    d_qkv.reverse()
    total_qkv = both_cores(mixed_attn, d_qkv)
    d_qkv, total_qkv = lax.optimization_barrier((d_qkv, total_qkv))
    d_mixed_attn = grouped(sum(dot(d, w, NT) for d, w in zip(d_qkv, qkv_ws)))
    d_shift_attn = jnp.sum(d_mixed_attn, axis=1)
    d_scale_attn = jnp.sum(d_mixed_attn * norm_attn, axis=1)
    grad_rows = flat(
        (d_middle + norm_back(norm_attn, inv_attn, d_mixed_attn * (1.0 + scale_attn))).astype(bf16)
    )

    def give(x):
        if not pair:
            return jnp.swapaxes(x.reshape(slots, rows, width), 0, 1)
        mine, other, last = x[:rows], swap_tensor(x[rows : 2 * rows]), x[2 * rows :]
        return jnp.stack(
            [jnp.where(t == 0, mine, other), jnp.where(t == 0, other, mine), last], axis=1
        )

    out_tokens = give(out_rows)
    grad_tokens = give(grad_rows)

    def scatter_weight(total, kinds, wide):
        part = lax.optimization_barrier(
            lax.psum_scatter(total, "dpo", scatter_dimension=0, tiled=True)
        )
        part = part[:, : kinds * tsize * wide].reshape(2 * drows, kinds, tsize, wide)
        if tsize == 2:
            met = swap_tensor(at(part, 1 - t, 2))
            part = at(part, t, 2).astype(f32) + met.astype(f32)
        else:
            part = lax.psum_scatter(part.astype(f32), "tensor", scatter_dimension=2, tiled=True)
            part = part.reshape(2 * drows, kinds, wide)
        part = part.reshape(2, drows, kinds, 1, wide)
        mine = at(part, c, 0)
        met = swap_core(at(part, 1 - c, 0))
        return in_order(c, mine, met, 2).reshape(drows, kinds, 2 * wide)

    grad_w_fc1 = scatter_weight(total_fc1, 1, fc_w).reshape(drows, 2 * fc_w)
    grad_w_fc2 = scatter_weight(total_fc2, 1, fc_w).reshape(drows, 2 * fc_w).T
    grad_w_out = scatter_weight(total_out, 1, head_w).reshape(drows, slab).T
    grad_w_qkv = scatter_weight(total_qkv, 3, head_w)

    d_mod_groups = jnp.stack(
        [d_shift_attn, d_scale_attn, d_gate_attn, d_shift_mlp, d_scale_mlp, d_gate_mlp], axis=1
    )
    d_mod = jnp.sum(
        jnp.where(slot_pick[:, :, None, None], d_mod_groups[:, None], 0.0), axis=0
    )

    def bias_back(halves, wide):
        own, other = (x.reshape(x.shape[0], tsize, 1, wide) for x in halves)
        return in_order(c, own, other, 2).reshape(own.shape[0], tsize, 2 * wide)

    d_bias_q = [jnp.sum(d[:, :hslab].astype(f32), axis=0) for d in d_qkv]
    d_bias_v = [jnp.sum(d[:, 2 * hslab : 3 * hslab].astype(f32), axis=0) for d in d_qkv]
    d_bias_qv = bias_back([jnp.stack([q, v]) for q, v in zip(d_bias_q, d_bias_v)], head_w)
    d_bias_fc = bias_back([x[None] for x in d_bias_fc1], fc_w)
    d_bias_out = jnp.stack(
        [jnp.sum(d_branch_attn.astype(f32), axis=0), jnp.sum(d_branch_mlp.astype(f32), axis=0)]
    ).reshape(2, tsize, slab)
    small = jnp.concatenate(
        [
            jnp.swapaxes(d_mod.reshape(slots * 6, tsize, slab), 0, 1).reshape(tsize, -1),
            jnp.swapaxes(d_bias_qv, 0, 1).reshape(tsize, -1),
            jnp.swapaxes(d_bias_fc, 0, 1).reshape(tsize, -1),
            jnp.swapaxes(d_bias_out, 0, 1).reshape(tsize, -1),
        ],
        axis=1,
    )
    if tsize == 2:
        small = at(small, t, 0) + swap_tensor(at(small, 1 - t, 0))
    else:
        small = lax.psum_scatter(small, "tensor", scatter_dimension=0, tiled=True)[0]
    every = lax.all_gather(small, ("dpo", "core"), axis=0, tiled=False)
    mod_size = slots * 6 * slab
    mod_all = every[:, :mod_size].reshape(dp_size * slots, 6 * slab)
    bias_sum = jnp.sum(every[:, mod_size:], axis=0)
    d_ada_bias = jnp.sum(mod_all, axis=0)
    grad_w_ada = lax.dot_general(
        silu_slots.astype(f32), mod_all, TN, precision=lax.Precision.HIGHEST
    ).reshape(drows, 6, slab)
    d_silu_slots = lax.dot_general(
        mod_all, ada_flat.astype(f32), NT, precision=lax.Precision.HIGHEST
    )
    d_silu = lax.dot_general(picker_live, d_silu_slots, TN, precision=lax.Precision.HIGHEST)
    _, silu_back = jax.vjp(jax.nn.silu, cond_here)
    cond_part = silu_back(d_silu)[0].reshape(-1)
    shared = jnp.concatenate([d_ada_bias, bias_sum])
    share = shared.shape[0] // dp_size
    shared_part = lax.dynamic_slice_in_dim(shared, r * share, share, 0)
    mine = jnp.concatenate([cond_part, shared_part])
    mine = jnp.pad(mine, (0, -mine.shape[0] % (8 * LANES))).reshape(1, -1, LANES)
    last = lax.all_gather(mine, ("dpo", "core", "tensor"), axis=0, tiled=True)
    last = last.reshape(dp_size, tsize, -1)
    cond_size = latents * drows
    grad_cond = jnp.sum(last[:, :, :cond_size], axis=1).reshape(dp_size, latents, drows)
    grad_cond = jnp.swapaxes(grad_cond, 0, 1).reshape(latents, width)
    spread = jnp.swapaxes(last[:, :, cond_size : cond_size + share], 0, 1)
    spread = spread.reshape(tsize, dp_size * share)

    def whole(start, kinds, wide):
        part = spread[:, start : start + kinds * wide].reshape(tsize, kinds, wide)
        return jnp.swapaxes(part, 0, 1).reshape(kinds, tsize * wide)

    grad_b_ada = whole(0, 6, slab)
    grad_b_qv = whole(6 * slab, 2, slab)
    grad_b_fc1 = whole(8 * slab, 1, 2 * fc_w)[0]
    grad_b_out2 = whole(8 * slab + 2 * fc_w, 2, slab)
    return (
        out_tokens,
        grad_tokens,
        grad_cond,
        grad_w_ada,
        grad_b_ada,
        grad_w_qkv,
        grad_b_qv,
        grad_w_out,
        grad_w_fc1,
        grad_b_fc1,
        grad_w_fc2,
        grad_b_out2,
    )


def solution(mesh):
    dp_size, tensor_size = mesh.devices.shape
    split = Mesh(mesh.devices.reshape(dp_size // 2, 2, tensor_size), ("dpo", "core", "tensor"))
    dp = ("dpo", "core")
    placed = (
        P("tensor", dp, None),
        P(),
        P("tensor", dp, None),
        P(),
        P(),
        P(dp, None, "tensor"),
        P(),
        P(dp, None, "tensor"),
        P(),
        P("tensor", dp),
        P(dp, "tensor"),
        P(),
        P("tensor", dp),
        P(),
    )
    return jax.shard_map(
        per_device,
        mesh=split,
        in_specs=placed,
        out_specs=(
            P("tensor", dp, None),
            P("tensor", dp, None),
            P(),
            P(dp, None, "tensor"),
            P(),
            P(dp, None, "tensor"),
            P(),
            P("tensor", dp),
            P(dp, "tensor"),
            P(),
            P("tensor", dp),
            P(),
        ),
        check_vma=False,
    )
```

```python
from functools import partial

import jax
import jax.numpy as jnp
import numpy as np
from jax import lax
from jax.experimental import pallas as pl
from jax.experimental.pallas import tpu as pltpu
from jax.sharding import Mesh
from jax.sharding import PartitionSpec as P

HEADS = 16
HEAD_DIM = 72
EPSILON = 1e-06
WINDOW = 256
LANES = 128
LOG2E = 1.4426950408889634
SQRT_2_PI = 0.7978845608028654
VMEM_BYTES = 56 * 2**20
SMALL_COST = pl.CostEstimate(flops=10**9, bytes_accessed=10**6, transcendentals=0)

NN = (((1,), (0,)), ((), ()))
NT = (((1,), (1,)), ((), ()))
TN = (((0,), (0,)), ((), ()))


def dot(left, right, dims=NN):
    return lax.dot_general(left, right, dims, preferred_element_type=jnp.float32)


def norm_parts(values):
    center = values - jnp.mean(values, axis=-1, keepdims=True)
    spread = jnp.mean(center * center, axis=-1, keepdims=True)
    inverse = lax.rsqrt(spread + EPSILON)
    return center * inverse, inverse


def norm_back(normed, inverse, grad):
    mean_grad = jnp.mean(grad, axis=-1, keepdims=True)
    mean_prod = jnp.mean(grad * normed, axis=-1, keepdims=True)
    return (grad - mean_grad - normed * mean_prod) * inverse


def round_up(value, step):
    return -(-value // step) * step


def window(column, width):
    start = jnp.minimum((column // LANES) * LANES, width - WINDOW)
    low = column - start
    lane = lax.broadcasted_iota(jnp.int32, (1, WINDOW), 1)
    return pl.ds(pl.multiple_of(start, LANES), WINDOW), (lane >= low) & (lane < low + HEAD_DIM)


def forward_kernel(k_at, v_at, chunk, q_ref, kv_ref, o_ref, log_ref):
    head = pl.program_id(0)
    column = head * HEAD_DIM
    q_cols, _ = window(column, q_ref.shape[1])
    k_cols, _ = window(k_at + column, kv_ref.shape[1])
    v_cols, v_mask = window(v_at + column, kv_ref.shape[1])
    o_cols, o_mask = window(column, o_ref.shape[1])

    @pl.when(head == 0)
    def _():
        o_ref[...] = jnp.zeros_like(o_ref)

    keys = align_head(kv_ref[:, k_cols], k_at + column, kv_ref.shape[1], column, q_ref.shape[1])
    values = align_head(kv_ref[:, v_cols], v_at + column, kv_ref.shape[1], column, o_ref.shape[1])
    factor = HEAD_DIM ** (-0.5) * LOG2E
    for part in range(q_ref.shape[0] // chunk):
        rows = pl.ds(part * chunk, chunk)
        scores = dot(keys, q_ref[rows, q_cols], NT)
        peak = jnp.max(scores, axis=0, keepdims=True)
        expo = jnp.exp2((scores - peak) * factor)
        total = jnp.sum(expo, axis=0, keepdims=True)
        mixed = dot(values, expo.astype(jnp.bfloat16), TN) * (1.0 / total)
        o_ref[rows, o_cols] = o_ref[rows, o_cols] + mixed.T.astype(jnp.bfloat16)
        log_ref[pl.ds(head, 1), rows] = peak * factor + jnp.log2(total)


def align_head(block, from_column, from_width, to_column, to_width):
    from_start = jnp.minimum((from_column // LANES) * LANES, from_width - WINDOW)
    to_start = jnp.minimum((to_column // LANES) * LANES, to_width - WINDOW)
    from_low = from_column - from_start
    to_low = to_column - to_start
    shift = lax.rem(to_low - from_low + WINDOW, WINDOW)
    lane = lax.broadcasted_iota(jnp.int32, (1, WINDOW), 1)
    moved = pltpu.roll(block.astype(jnp.float32), shift, 1)
    keep = (lane >= to_low) & (lane < to_low + HEAD_DIM)
    return jnp.where(keep, moved, 0.0).astype(jnp.bfloat16)


def backward_kernel(k_at, v_at, dk_at, dv_at, chunk, joined, q_ref, kv_ref, do_ref, log_ref, *outs):
    head = pl.program_id(0)
    column = head * HEAD_DIM
    if joined:
        (dq_ref,) = outs
        dkv_ref = dq_ref
    else:
        dq_ref, dkv_ref = outs
    q_cols, q_mask = window(column, q_ref.shape[1])
    k_cols, _ = window(k_at + column, kv_ref.shape[1])
    v_cols, _ = window(v_at + column, kv_ref.shape[1])
    do_cols, _ = window(column, do_ref.shape[1])
    dq_cols, dq_mask = window(column, dq_ref.shape[1])
    dk_cols, dk_mask = window(dk_at + column, dkv_ref.shape[1])
    dv_cols, dv_mask = window(dv_at + column, dkv_ref.shape[1])

    @pl.when(head == 0)
    def _():
        for out in outs:
            out[...] = jnp.zeros_like(out)

    width = q_ref.shape[1]
    keys = align_head(kv_ref[:, k_cols], k_at + column, kv_ref.shape[1], column, width)
    values = align_head(kv_ref[:, v_cols], v_at + column, kv_ref.shape[1], column, do_ref.shape[1])
    scale = HEAD_DIM ** (-0.5)
    factor = scale * LOG2E
    dk_total = jnp.zeros((kv_ref.shape[0], WINDOW), jnp.float32)
    dv_total = jnp.zeros((kv_ref.shape[0], WINDOW), jnp.float32)
    for part in range(q_ref.shape[0] // chunk):
        rows = pl.ds(part * chunk, chunk)
        query = q_ref[rows, q_cols]
        grad = do_ref[rows, do_cols]
        scores = dot(keys, query, NT)
        probs = jnp.exp2(scores * factor - log_ref[pl.ds(head, 1), rows])
        d_probs = dot(values, grad, NT)
        inner = jnp.sum(d_probs * probs, axis=0, keepdims=True)
        d_scores = (probs * (d_probs - inner)).astype(jnp.bfloat16)
        dv_total = dv_total + dot(probs.astype(jnp.bfloat16), grad)
        dk_total = dk_total + dot(d_scores, query)
        d_query = (dot(keys, d_scores, TN) * scale).T
        moved = move_head(d_query, column, width, column, dq_ref.shape[1])
        dq_ref[rows, dq_cols] = dq_ref[rows, dq_cols] + moved
    dk_ref_add(dkv_ref, dk_cols, move_head(dk_total * scale, column, width, dk_at + column, dkv_ref.shape[1]))
    dk_ref_add(dkv_ref, dv_cols, move_head(dv_total, column, do_ref.shape[1], dv_at + column, dkv_ref.shape[1]))


def dk_ref_add(ref, cols, values):
    ref[:, cols] = ref[:, cols] + values


def move_head(block, from_column, from_width, to_column, to_width):
    return align_head(block, from_column, from_width, to_column, to_width)


def spec(shape, *index):
    return pl.BlockSpec(shape, lambda head: index, pipeline_mode=pl.Buffered(1))


def attend_forward(q, q_block, kv, kv_block, k_at, v_at, rows, keys, heads):
    width = round_up(heads * HEAD_DIM, LANES)
    return pl.pallas_call(
        partial(forward_kernel, k_at, v_at, min(256, rows)),
        grid=(heads,),
        in_specs=[
            spec((rows, q.shape[1]), q_block, 0),
            spec((keys, kv.shape[1]), kv_block, 0),
        ],
        out_specs=[spec((rows, width), 0, 0), spec((heads, rows), 0, 0)],
        out_shape=[
            jax.ShapeDtypeStruct((rows, width), jnp.bfloat16),
            jax.ShapeDtypeStruct((heads, rows), jnp.float32),
        ],
        compiler_params=pltpu.CompilerParams(vmem_limit_bytes=VMEM_BYTES),
        cost_estimate=pl.CostEstimate(
            flops=4 * heads * rows * keys * WINDOW,
            bytes_accessed=2 * (rows + keys) * 1792,
            transcendentals=heads * rows * keys,
        ),
        name="attend_forward",
    )(q, kv)


def attend_backward(q, q_block, kv, kv_block, k_at, v_at, grad, grad_block, log_total, rows, keys, heads, joined):
    slab = heads * HEAD_DIM
    if joined:
        out_specs = [spec((rows, q.shape[1]), 0, 0)]
        out_shape = [jax.ShapeDtypeStruct((rows, q.shape[1]), jnp.bfloat16)]
        dk_at, dv_at = k_at, v_at
    else:
        width = round_up(slab, LANES)
        out_specs = [spec((rows, width), 0, 0), spec((keys, 2 * slab), 0, 0)]
        out_shape = [
            jax.ShapeDtypeStruct((rows, width), jnp.bfloat16),
            jax.ShapeDtypeStruct((keys, 2 * slab), jnp.bfloat16),
        ]
        dk_at, dv_at = 0, slab
    return pl.pallas_call(
        partial(backward_kernel, k_at, v_at, dk_at, dv_at, min(256, rows), joined),
        grid=(heads,),
        in_specs=[
            spec((rows, q.shape[1]), q_block, 0),
            spec((keys, kv.shape[1]), kv_block, 0),
            spec((rows, grad.shape[1]), grad_block, 0),
            spec((heads, rows), 0, 0),
        ],
        out_specs=out_specs,
        out_shape=out_shape,
        compiler_params=pltpu.CompilerParams(vmem_limit_bytes=VMEM_BYTES),
        cost_estimate=SMALL_COST,
        name="attend_backward",
    )(q, kv, grad, log_total)


def mlp_kernel(x_ref, g_ref, w1_ref, w2_ref, b_ref, hidden_ref, d_ref, bias_ref):
    value = dot(x_ref[...], w1_ref[...]) + b_ref[...]
    grad = dot(g_ref[...], w2_ref[...])
    square = value * value
    curve = jnp.tanh(SQRT_2_PI * value * (1.0 + 0.044715 * square))
    left = 0.5 + 0.5 * curve
    hidden_ref[...] = (value * left).astype(jnp.bfloat16)
    slope = left + (0.5 * SQRT_2_PI) * value * (1.0 - curve * curve) * (1.0 + 0.134145 * square)
    d_pre = (grad * slope).astype(jnp.bfloat16)
    d_ref[...] = d_pre
    sums = jnp.sum(d_pre.astype(jnp.float32), axis=0, keepdims=True)

    @pl.when(pl.program_id(1) == 0)
    def _():
        bias_ref[...] = sums

    @pl.when(pl.program_id(1) != 0)
    def _():
        bias_ref[...] = bias_ref[...] + sums


def mlp_middle(x, grad, w1, w2, bias):
    count, width = x.shape
    wide = bias.shape[0]
    rows = count // 3 if (count // 3) % 16 == 0 else count
    cols = wide // 3 if (wide // 3) % LANES == 0 else wide
    by_row = pl.BlockSpec((rows, width), lambda j, i: (i, 0))
    by_col = pl.BlockSpec((width, cols), lambda j, i: (0, j))
    by_both = pl.BlockSpec((rows, cols), lambda j, i: (i, j))
    one_row = pl.BlockSpec((1, cols), lambda j, i: (0, j))
    hidden, d_pre, sums = pl.pallas_call(
        mlp_kernel,
        grid=(wide // cols, count // rows),
        in_specs=[by_row, by_row, by_col, by_col, one_row],
        out_specs=[by_both, by_both, one_row],
        out_shape=[
            jax.ShapeDtypeStruct((count, wide), jnp.bfloat16),
            jax.ShapeDtypeStruct((count, wide), jnp.bfloat16),
            jax.ShapeDtypeStruct((1, wide), jnp.float32),
        ],
        compiler_params=pltpu.CompilerParams(vmem_limit_bytes=VMEM_BYTES),
        cost_estimate=pl.CostEstimate(
            flops=4 * count * width * wide,
            bytes_accessed=4 * (count + wide) * width + 4 * count * wide,
            transcendentals=count * wide,
        ),
        name="mlp_middle",
    )(x, grad, w1, w2, bias[None])
    return hidden, d_pre, sums[0]


def back_kernel(a0_ref, a1_ref, w0_ref, w1_ref, x_ref, base_ref, scale_ref, out_ref, sum_ref, prod_ref):
    grad = dot(a0_ref[...], w0_ref[...], NT) + dot(a1_ref[...], w1_ref[...], NT)
    normed, inverse = norm_parts(x_ref[...].astype(jnp.float32))
    back = norm_back(normed, inverse, grad * (1.0 + scale_ref[0]))
    out_ref[...] = (base_ref[...] + back).astype(out_ref.dtype)
    sums = jnp.sum(grad, axis=0, keepdims=True)
    prods = jnp.sum(grad * normed, axis=0, keepdims=True)

    @pl.when(pl.program_id(1) == 0)
    def _():
        sum_ref[0] = sums
        prod_ref[0] = prods

    @pl.when(pl.program_id(1) != 0)
    def _():
        sum_ref[0] = sum_ref[0] + sums
        prod_ref[0] = prod_ref[0] + prods


def matmul_norm_back(halves, weights, deep, x, base, scale, kind):
    count, width = x.shape
    groups = scale.shape[0]
    rows = count // groups
    block = 256 if rows % 256 == 0 else rows
    steps = rows // block

    def by_row(wide):
        return pl.BlockSpec((block, wide), lambda g, i: (g * steps + i, 0))

    weight = pl.BlockSpec((width, deep), lambda g, i: (0, 0), pipeline_mode=pl.Buffered(1))
    one_row = pl.BlockSpec((1, 1, width), lambda g, i: (g, 0, 0))
    one_sum = jax.ShapeDtypeStruct((groups, 1, width), jnp.float32)
    out, sums, prods = pl.pallas_call(
        back_kernel,
        grid=(groups, steps),
        in_specs=[by_row(deep), by_row(deep), weight, weight, by_row(width), by_row(width), one_row],
        out_specs=[by_row(width), one_row, one_row],
        out_shape=[jax.ShapeDtypeStruct((count, width), kind), one_sum, one_sum],
        compiler_params=pltpu.CompilerParams(vmem_limit_bytes=VMEM_BYTES),
        cost_estimate=SMALL_COST,
        name="matmul_norm_back",
    )(halves[0], halves[1], weights[0], weights[1], x, base, scale)
    return out, sums[:, 0], prods[:, 0]


def per_device(
    tokens,
    conditioning,
    cotangent,
    latent_counts,
    latent_order,
    w_ada,
    b_ada,
    w_qkv,
    b_qv,
    w_out,
    w_fc1,
    b_fc1,
    w_fc2,
    b_out2,
):
    tsize = lax.axis_size("tensor")
    t = lax.axis_index("tensor")
    c = lax.axis_index("core")
    r = lax.axis_index("dpo") * 2 + c
    dp_size = lax.axis_size("dpo") * 2
    f32, bf16 = jnp.float32, jnp.bfloat16
    rows, slots, width = tokens.shape
    latents = conditioning.shape[0]
    drows = w_ada.shape[0]
    slab = width // tsize
    half_heads = HEADS // 2
    hslab = half_heads * HEAD_DIM
    head_w = slab // 2
    fc_w = w_fc1.shape[1] // 2
    qkv_w = round_up(3 * hslab, LANES)
    out_w = round_up(hslab, LANES)
    pair = tsize == 2 and slots == 3

    def swap_core(x):
        return lax.ppermute(x, "core", [(0, 1), (1, 0)])

    def swap_tensor(x):
        return lax.ppermute(x, "tensor", [(0, 1), (1, 0)])

    def in_order(index, mine, other, axis):
        first = jnp.where(index == 0, mine, other)
        second = jnp.where(index == 0, other, mine)
        return jnp.concatenate([first, second], axis=axis)

    def at(x, index, axis):
        return lax.dynamic_index_in_dim(x, index, axis, keepdims=False)

    bits = [("core", 0)]
    while 2 ** len(bits) < dp_size:
        bits.append(("dpo", len(bits) - 1))
    dpo_size = dp_size // 2

    def hop(x, axis, bit):
        size = 2 if axis == "core" else dpo_size
        return lax.ppermute(x, axis, [(i, i ^ (1 << bit)) for i in range(size)])

    def bit_of(axis, bit):
        return (lax.axis_index(axis) >> bit) & 1

    def sum_scatter_dp(x):
        for axis, bit in bits:
            x = x.reshape((x.shape[0] // 2, 2) + x.shape[1:])
            here = bit_of(axis, bit)
            x = at(x, here, 1) + hop(at(x, 1 - here, 1), axis, bit)
        return x[0]

    def gather_dp(x, tie=None):
        x = x[None]
        for step, (axis, bit) in enumerate(reversed(bits)):
            if step == 1 and tie is not None:
                x, tie = lax.optimization_barrier((x, tie))
            here = bit_of(axis, bit)
            other = hop(x, axis, bit)
            x = jnp.stack([jnp.where(here == 0, x, other), jnp.where(here == 0, other, x)], axis=1)
            x = x.reshape((-1,) + x.shape[2:])
        return x if tie is None else (x, tie)

    def sum_tensor(x):
        if tsize == 2:
            return at(x, t, 0) + swap_tensor(at(x, 1 - t, 0))
        return lax.psum_scatter(x, "tensor", scatter_dimension=0, tiled=True)[0]

    def all_tensor(x):
        if tsize == 2:
            return in_order(t, x[None], swap_tensor(x)[None], 0)
        return lax.all_gather(x, "tensor", axis=0, tiled=False)

    starts = jnp.cumsum(latent_counts) - latent_counts
    slot_all = jnp.arange(slots * dp_size, dtype=jnp.int32)
    owner, within = slot_all // slots, slot_all % slots
    live_all = (within < latent_counts[owner]).astype(f32)
    chosen = latent_order[jnp.clip(starts[owner] + within, 0, latents - 1)]
    picker = (chosen[:, None] == jnp.arange(latents, dtype=jnp.int32)[None, :]).astype(f32)
    picker_live = picker * live_all[:, None]
    cond_here = lax.dynamic_slice_in_dim(conditioning, r * drows, drows, 1).astype(f32)
    silu_here = jax.nn.silu(cond_here).astype(bf16)
    silu_slots = jnp.dot(picker, silu_here.astype(f32), precision=lax.Precision.HIGHEST).astype(bf16)

    ada_flat = w_ada.reshape(drows, 6 * slab)
    mod_part = dot(silu_slots, ada_flat).reshape(dp_size, slots * 6, slab)
    mod_here = sum_scatter_dp(mod_part).reshape(slots, 6, slab)
    if tsize == 2:
        modulation = in_order(t, mod_here, swap_tensor(mod_here), 2)
    else:
        modulation = lax.all_gather(mod_here, "tensor", axis=2, tiled=True)
    modulation = modulation + b_ada.astype(f32)[None]

    if pair:

        def take(x):
            mine = at(x, t, 1)
            other = swap_tensor(at(x, 1 - t, 1))
            return jnp.concatenate([mine, other, x[:, 2]], axis=0)

        group_slots = jnp.stack([t, t, jnp.full_like(t, 2)])
    else:

        def take(x):
            return jnp.swapaxes(x, 0, 1).reshape(slots * rows, width)

        group_slots = jnp.arange(slots, dtype=jnp.int32)
    groups = slots
    count = groups * rows
    tokens_in = take(tokens)
    cot_in = take(cotangent)
    slot_pick = group_slots[:, None] == jnp.arange(slots, dtype=jnp.int32)[None, :]
    live_here = lax.dynamic_slice_in_dim(live_all, r * slots, slots, 0)
    live = jnp.sum(jnp.where(slot_pick, live_here[None], 0.0), axis=1)
    mod_groups = jnp.sum(
        jnp.where(slot_pick[:, :, None, None], modulation[None], 0.0), axis=1
    )

    def grouped(x):
        return x.reshape(groups, rows, x.shape[-1])

    def flat(x):
        return x.reshape(count, x.shape[-1])

    shift_attn, scale_attn, gate_attn, shift_mlp, scale_mlp, gate_mlp = (
        mod_groups[:, i][:, None, :] for i in range(6)
    )

    shards = (
        w_qkv.reshape(drows, 3, 2, head_w),
        w_out.T.reshape(drows, 1, 2, head_w),
        w_fc1.reshape(drows, 1, 2, fc_w),
        w_fc2.T.reshape(drows, 1, 2, fc_w),
    )
    pads = (qkv_w - 3 * hslab, out_w - hslab, 0, 0)

    def quad(some):
        def side(which):
            parts = [at(x, which, 2).reshape(drows, -1) for x in some]
            return parts[0] if len(parts) == 1 else jnp.concatenate(parts, axis=1)

        both = in_order(c, side(c), swap_core(side(1 - c)), 0)
        if tsize == 2:
            met = swap_tensor(both)
            return [jnp.where(t == 0, both, met), jnp.where(t == 0, met, both)]
        met = lax.all_gather(both, "tensor", axis=0, tiled=False)
        return [met[i] for i in range(tsize)]

    def columns(by_tensor, offset, kinds, wide, pad):
        parts = [
            y[:, offset : offset + kinds * wide].reshape(2 * drows, kinds, 1, wide) for y in by_tensor
        ]
        joined = jnp.concatenate(parts, axis=2).reshape(2 * drows, kinds * tsize * wide)
        return jnp.pad(joined, ((0, 0), (0, pad))) if pad else joined

    def gather(x):
        own = lax.all_gather(x, "dpo", axis=0, tiled=True)
        return own, swap_core(own)

    qkv_ws = gather(columns(quad(shards[:1]), 0, 3, head_w, pads[0]))
    rest = quad(shards[1:])
    out_fc1 = jnp.concatenate(
        [columns(rest, head_w, 1, fc_w, 0), columns(rest, 0, 1, head_w, pads[1])], axis=1
    )
    out_fc1_ws = gather(out_fc1)
    fc_all = fc_w * tsize
    out_ws = [w[:, fc_all:] for w in out_fc1_ws]
    first_w, fc2_cols = lax.optimization_barrier(
        (qkv_ws[0], columns(rest, head_w + fc_w, 1, fc_w, 0))
    )
    qkv_ws = (first_w, qkv_ws[1])
    fc2_own = lax.all_gather(fc2_cols, "dpo", axis=0, tiled=True)

    def bias_halves(bias, wide):
        parts = bias.astype(f32).reshape(bias.shape[0], tsize, 2, wide)
        return [at(parts, which, 2).reshape(bias.shape[0], tsize * wide) for which in (c, 1 - c)]

    qv_halves = bias_halves(b_qv, head_w)
    qkv_bias = [
        jnp.concatenate(
            [b[0], jnp.zeros((hslab,), f32), b[1], jnp.zeros((pads[0],), f32)]
        )
        for b in qv_halves
    ]
    fc1_bias = [b[0] for b in bias_halves(b_fc1[None], fc_w)]
    bias_attn_out, bias_mlp_out = b_out2[0].astype(f32), b_out2[1].astype(f32)

    x_in = grouped(tokens_in.astype(f32))
    norm_attn, inv_attn = norm_parts(x_in)
    mixed_attn = flat((norm_attn * (1.0 + scale_attn) + shift_attn).astype(bf16))
    qkv = [(dot(mixed_attn, w) + b).astype(bf16) for w, b in zip(qkv_ws, qkv_bias)]

    if pair:
        segments = [(2, 1)]
    else:
        segments = [(g, 1) for g in range(groups)]
    seq = rows * tsize

    def gather_keys(x):
        if tsize == 2:
            return jnp.concatenate([x, swap_tensor(x)], axis=0)
        return lax.all_gather(x, "tensor", axis=0, tiled=True)

    def scatter_keys(x):
        if tsize == 2:
            return (x[:rows].astype(f32) + swap_tensor(x[rows:]).astype(f32)).astype(bf16)
        return lax.psum_scatter(x.astype(f32), "tensor", scatter_dimension=0, tiled=True).astype(bf16)

    mixed_parts, log_parts, key_parts = [], [], []
    for x in qkv:
        keys_by_segment = [
            gather_keys(x[g * rows : (g + 1) * rows, hslab : 3 * hslab]) for g, _ in segments
        ]
        outs, logs = [], []
        if pair:
            out, log = attend_forward(x, 0, x, 0, hslab, 2 * hslab, seq, seq, half_heads)
            outs.append(out)
            logs.append(log)
        for (g, _), kv in zip(segments, keys_by_segment):
            out, log = attend_forward(x, g, kv, 0, 0, hslab, rows, seq, half_heads)
            outs.append(out)
            logs.append(log)
        mixed_parts.append(jnp.concatenate(outs, axis=0))
        log_parts.append(logs)
        key_parts.append(keys_by_segment)
    fc2_own, mixed_parts = lax.optimization_barrier((fc2_own, mixed_parts))
    fc2_ws = (fc2_own, swap_core(fc2_own))
    branch_attn = grouped(
        sum(dot(x, w, NT) for x, w in zip(mixed_parts, out_ws)) + bias_attn_out
    )
    middle = x_in + gate_attn * branch_attn
    norm_mlp, inv_mlp = norm_parts(middle)
    mixed_mlp = flat((norm_mlp * (1.0 + scale_mlp) + shift_mlp).astype(bf16))

    grad_out = grouped(cot_in.astype(f32)) * live[:, None, None]
    d_branch_mlp = flat((grad_out * gate_mlp).astype(bf16))
    hidden, d_pre, d_bias_fc1 = [], [], []
    for w1, w2, b in zip(out_fc1_ws, fc2_ws, fc1_bias):
        act, d_act, d_b = mlp_middle(mixed_mlp, d_branch_mlp, w1, w2, b)
        hidden.append(act)
        d_pre.append(d_act)
        d_bias_fc1.append(d_b)

    def both_cores(left, rights):
        met = swap_core(dot(left, rights[1], TN).astype(bf16))
        return (dot(left, rights[0], TN).astype(bf16).astype(f32) + met.astype(f32)).astype(bf16)

    def scatter_dpo(total):
        return lax.optimization_barrier(
            lax.psum_scatter(total, "dpo", scatter_dimension=0, tiled=True)
        )

    total_fc2 = both_cores(d_branch_mlp, hidden)
    total_fc1 = both_cores(mixed_mlp, d_pre)
    hidden, d_pre, total_fc1, total_fc2 = lax.optimization_barrier(
        (hidden, d_pre, total_fc1, total_fc2)
    )
    branch_mlp = grouped(sum(dot(h, w, NT) for h, w in zip(hidden, fc2_ws)) + bias_mlp_out)
    out_rows = flat(((middle + gate_mlp * branch_mlp) * live[:, None, None]).astype(bf16))
    d_gate_mlp = jnp.sum(grad_out * branch_mlp, axis=1)
    d_middle, d_shift_mlp, d_scale_mlp = matmul_norm_back(
        d_pre, out_fc1_ws, fc_all, flat(middle), flat(grad_out), scale_mlp, f32
    )
    d_middle = grouped(d_middle)
    d_branch_attn = flat((d_middle * gate_attn).astype(bf16))
    d_gate_attn = jnp.sum(d_middle * branch_attn, axis=1)

    total_out = both_cores(d_branch_attn, mixed_parts)
    total_fc1_out = jnp.concatenate([total_fc1, total_out], axis=1)
    d_branch_attn, total_fc1_out = lax.optimization_barrier((d_branch_attn, total_fc1_out))
    part_fc2, part_fc1_out = scatter_dpo(total_fc2), scatter_dpo(total_fc1_out)
    d_qkv = []
    for x, w, logs, keys_by_segment in reversed(list(zip(qkv, out_ws, log_parts, key_parts))):
        d_mixed = dot(d_branch_attn, w).astype(bf16)
        d_rows = []
        first = 1 if pair else 0
        for i, (g, _) in enumerate(segments):
            d_q, d_kv = attend_backward(
                x, g, keys_by_segment[i], 0, 0, hslab, d_mixed, g, logs[first + i], rows, seq, half_heads, False
            )
            d_rows.append(
                jnp.concatenate(
                    [d_q[:, :hslab], scatter_keys(d_kv), jnp.zeros((rows, pads[0]), bf16)], axis=1
                )
            )
        if pair:
            (whole,) = attend_backward(
                x, 0, x, 0, hslab, 2 * hslab, d_mixed, 0, logs[0], seq, seq, half_heads, True
            )
            d_rows.insert(0, whole)
        d_qkv.append(jnp.concatenate(d_rows, axis=0))
    d_qkv.reverse()
    d_qkv, part_fc2, part_fc1_out = lax.optimization_barrier((d_qkv, part_fc2, part_fc1_out))
    total_qkv = both_cores(mixed_attn, d_qkv)
    d_qkv, total_qkv = lax.optimization_barrier((d_qkv, total_qkv))
    grad_rows, d_shift_attn, d_scale_attn = matmul_norm_back(
        d_qkv, qkv_ws, qkv_w, tokens_in, flat(d_middle), scale_attn, bf16
    )

    def give(x):
        if not pair:
            return jnp.swapaxes(x.reshape(slots, rows, width), 0, 1)
        mine, other, last = x[:rows], swap_tensor(x[rows : 2 * rows]), x[2 * rows :]
        return jnp.stack(
            [jnp.where(t == 0, mine, other), jnp.where(t == 0, other, mine), last], axis=1
        )

    out_tokens = give(out_rows)
    grad_tokens = give(grad_rows)

    def finish_weight(part, kinds, wide):
        part = part[:, : kinds * tsize * wide].reshape(2 * drows, kinds, tsize, wide)
        if tsize == 2:
            met = swap_tensor(at(part, 1 - t, 2))
            part = at(part, t, 2).astype(f32) + met.astype(f32)
        else:
            part = lax.psum_scatter(part.astype(f32), "tensor", scatter_dimension=2, tiled=True)
            part = part.reshape(2 * drows, kinds, wide)
        part = part.reshape(2, drows, kinds, 1, wide)
        mine = at(part, c, 0)
        met = swap_core(at(part, 1 - c, 0))
        return in_order(c, mine, met, 2).reshape(drows, kinds, 2 * wide)

    def by_slot(parts):
        stacked = jnp.stack(parts, axis=1)
        return jnp.sum(jnp.where(slot_pick[:, :, None, None], stacked[:, None], 0.0), axis=0)

    def by_tensor_index(x):
        parts = x.reshape(-1, tsize, x.shape[-1] // tsize)
        return jnp.swapaxes(parts, 0, 1).reshape(tsize, -1)

    def bias_back(halves, wide):
        own, other = (x.reshape(x.shape[0], tsize, 1, wide) for x in halves)
        return in_order(c, own, other, 2).reshape(own.shape[0], tsize * 2 * wide)

    def shared(parts, tie=None):
        mine = sum_tensor(jnp.concatenate([by_tensor_index(x) for x in parts], axis=1))
        return gather_dp(mine, tie)

    d_bias_fc = bias_back([x[None] for x in d_bias_fc1], fc_w)
    d_bias_out = jnp.stack(
        [jnp.sum(d_branch_attn.astype(f32), axis=0), jnp.sum(d_branch_mlp.astype(f32), axis=0)]
    )
    early = shared(
        [by_slot([d_gate_attn, d_shift_mlp, d_scale_mlp, d_gate_mlp]), d_bias_fc, d_bias_out]
    )
    d_bias_q = [jnp.sum(d[:, :hslab].astype(f32), axis=0) for d in d_qkv]
    d_bias_v = [jnp.sum(d[:, 2 * hslab : 3 * hslab].astype(f32), axis=0) for d in d_qkv]
    d_bias_qv = bias_back([jnp.stack([q, v]) for q, v in zip(d_bias_q, d_bias_v)], head_w)
    late, part_qkv = shared(
        [by_slot([d_shift_attn, d_scale_attn]), d_bias_qv], scatter_dpo(total_qkv)
    )

    def split_mod(x, kinds):
        size = slots * kinds * slab
        return x[:, :size].reshape(dp_size * slots, kinds * slab), jnp.sum(x[:, size:], axis=0)

    mod_late, bias_late = split_mod(late, 2)
    mod_early, bias_early = split_mod(early, 4)
    silu_f32 = silu_slots.astype(f32)
    ada_f32 = ada_flat.astype(f32)

    def exact(left, right, dims):
        return lax.dot_general(left, right, dims, precision=lax.Precision.HIGHEST)

    grad_w_ada = jnp.concatenate(
        [exact(silu_f32, mod_late, TN), exact(silu_f32, mod_early, TN)], axis=1
    ).reshape(drows, 6, slab)
    d_silu_slots = exact(mod_late, ada_f32[:, : 2 * slab], NT) + exact(
        mod_early, ada_f32[:, 2 * slab :], NT
    )
    d_silu = exact(picker_live, d_silu_slots, TN)
    if tsize == 2:
        d_silu = d_silu + swap_tensor(d_silu)
    else:
        d_silu = lax.psum(d_silu, "tensor")
    _, silu_back = jax.vjp(jax.nn.silu, cond_here)
    grad_cond = jnp.swapaxes(gather_dp(silu_back(d_silu)[0]), 0, 1).reshape(latents, width)
    biases = all_tensor(
        jnp.concatenate([jnp.sum(mod_late, axis=0), jnp.sum(mod_early, axis=0), bias_late, bias_early])
    )

    def whole(start, kinds, wide):
        part = biases[:, start : start + kinds * wide].reshape(tsize, kinds, wide)
        return jnp.swapaxes(part, 0, 1).reshape(kinds, tsize * wide)

    grad_b_ada = whole(0, 6, slab)
    grad_b_qv = whole(6 * slab, 2, slab)
    grad_b_fc1 = whole(8 * slab, 1, 2 * fc_w)[0]
    grad_b_out2 = whole(8 * slab + 2 * fc_w, 2, slab)
    grad_w_fc1 = finish_weight(part_fc1_out[:, :fc_all], 1, fc_w).reshape(drows, 2 * fc_w)
    grad_w_fc2 = finish_weight(part_fc2, 1, fc_w).reshape(drows, 2 * fc_w).T
    grad_w_out = finish_weight(part_fc1_out[:, fc_all:], 1, head_w).reshape(drows, slab).T
    grad_w_qkv = finish_weight(part_qkv, 3, head_w)
    return (
        out_tokens,
        grad_tokens,
        grad_cond,
        grad_w_ada,
        grad_b_ada,
        grad_w_qkv,
        grad_b_qv,
        grad_w_out,
        grad_w_fc1,
        grad_b_fc1,
        grad_w_fc2,
        grad_b_out2,
    )


def solution(mesh):
    dp_size, tensor_size = mesh.devices.shape
    split = Mesh(mesh.devices.reshape(dp_size // 2, 2, tensor_size), ("dpo", "core", "tensor"))
    dp = ("dpo", "core")
    placed = (
        P("tensor", dp, None),
        P(),
        P("tensor", dp, None),
        P(),
        P(),
        P(dp, None, "tensor"),
        P(),
        P(dp, None, "tensor"),
        P(),
        P("tensor", dp),
        P(dp, "tensor"),
        P(),
        P("tensor", dp),
        P(),
    )
    return jax.shard_map(
        per_device,
        mesh=split,
        in_specs=placed,
        out_specs=(
            P("tensor", dp, None),
            P("tensor", dp, None),
            P(),
            P(dp, None, "tensor"),
            P(),
            P(dp, None, "tensor"),
            P(),
            P("tensor", dp),
            P(dp, "tensor"),
            P(),
            P("tensor", dp),
            P(),
        ),
        check_vma=False,
    )
```
